256 devices in a mesh: ctx: 128 (over x, z, y), head: 2 (over core).
Axes of the slice: x: 4, y: 4, z: 8, core: 2. Of those that a mesh axis runs over, the one named last changes fastest.
Arguments:
- shared_qk: bfloat16 [16384, 2048], P('ctx', 'head'), may hold values from -6 to 6
- values: bfloat16 [16384, 2048], P('ctx', 'head'), may hold values from -12 to 12
- out_grad: bfloat16 [16384, 2048], P('ctx', 'head'), may hold values from -6 to 6
- out_weight: bfloat16 [2048, 2048], P('ctx', 'head'), may hold values from -0.125 to 0.125
- buckets: int32 [2, 16384], P(None, 'ctx'), may hold values from 0 to 127, as said below
Outputs:
- mixed: bfloat16 [16384, 2048], P('ctx', 'head')
- grad_qk: bfloat16 [16384, 2048], P('ctx', 'head')
- grad_values: bfloat16 [16384, 2048], P('ctx', 'head')
- grad_weight: float32 [2048, 2048], P('ctx', 'head')
The draws below stay inside these ranges and needn't reach their ends.
Inputs may be any that keep to these rules, and one draw needn't show every extreme that they name: `buckets`: in each round at most 2 of the tokens of one device share a bucket, and one bucket takes exactly 2 tokens from every device.
All inputs are finite; a program needn't handle non-finite values.
Results may differ from the reference program's by a relative error of at most 0.012.
The reference program's roundings to bfloat16 on the way count: a program that leaves them out, or rounds other values in their place, can miss the bound.
Values may be sent and summed in bfloat16 or wider, within the bound.
No kernel may reach another device: no remote copies, remote signals or barrier semaphores. Data moves between devices by JAX's collectives and lax.ppermute only.
A program may use at most 128 MiB of HBM per device.

```python
import math
import jax
import jax.numpy as jnp
from jax import lax

D = 2048
HEADS = 16
HEAD_DIM = 128
ROUNDS = 2
SPAN = 128
TOK_DEV = 128
TOKENS = 16384
N_CTX = 128


def draw_shared_qk(key, part):
    key = jax.random.fold_in(key, 11)
    sample_rows = 1.4 * jax.random.normal(key, (TOKENS, D), jnp.float32)
    return jnp.clip(sample_rows, -6.0, 6.0).astype(jnp.bfloat16)


def draw_buckets(key, part):
    key = jax.random.fold_in(key, 7)
    owner_count = TOKENS // TOK_DEV
    per_peer = 2 * TOK_DEV // owner_count

    def one_source(source_key, busiest):
        order_key, slot_key = jax.random.split(source_key)
        shuffled = jax.random.permutation(order_key, TOK_DEV)
        spread = jax.random.permutation(slot_key, (owner_count - 1) * per_peer)[:TOK_DEV - per_peer] // per_peer
        spread = (spread + (spread >= busiest).astype(jnp.int32)).astype(jnp.int32)
        assigned = jnp.concatenate([jnp.full((per_peer,), busiest, jnp.int32), spread])
        return jnp.zeros((TOK_DEV,), jnp.int32).at[shuffled].set(assigned)

    def one_round(round_key):
        busy_key, source_root = jax.random.split(round_key)
        busiest = jax.random.randint(busy_key, (), 0, owner_count).astype(jnp.int32)
        source_keys = jax.random.split(source_root, owner_count)
        return jax.vmap(lambda source_key: one_source(source_key, busiest))(source_keys).reshape(TOKENS)
    return jax.vmap(one_round)(jax.random.split(key, ROUNDS)).astype(jnp.int32)


def steps_of(key, shape, shards, low, high):
    def one(dim, parts):
        draws = jax.random.uniform(jax.random.fold_in(jax.random.fold_in(key, 6), dim), (parts,), jnp.float32, low / len(shards), high / len(shards))
        return jnp.repeat(jnp.exp(draws), shape[dim] // parts).reshape((-1,) + (1,) * (len(shape) - dim - 1))

    loudness = one(*shards[0])
    for cut in shards[1:]:
        loudness = loudness * one(*cut)
    return loudness


def normal_values(own_key, shape, scale, limit, shards=(), kind=jnp.bfloat16):
    entries = scale * jax.random.normal(own_key, shape, jnp.float32)
    if shards:
        entries = entries * steps_of(own_key, shape, shards, -0.22, 0.18)
    return jnp.clip(entries, -limit, limit).astype(kind)


def setup_inputs(seed: int = 0) -> dict:
    streams_of = jax.random.split(jax.random.key(seed), 6)
    shared_qk = draw_shared_qk(jax.random.fold_in(streams_of[5], 71), 0)
    values = normal_values(streams_of[1], (TOKENS, D), 2.0, 12.0, ((0, 128), (1, 2)))
    out_grad = normal_values(streams_of[2], (TOKENS, D), 1.0, 6.0, ((0, 128), (1, 2)))
    out_weight = normal_values(streams_of[3], (D, D), D ** -0.5, 0.125, ((0, 128), (1, 2)))
    buckets = draw_buckets(jax.random.fold_in(streams_of[5], 71), 0)
    return dict(shared_qk=shared_qk, values=values, out_grad=out_grad, out_weight=out_weight, buckets=buckets)


self_penalty = 10000.0
masked_score = -1e+30
highest = lax.Precision.HIGHEST

def rounded(matrix):
    return lax.optimization_barrier(matrix.astype(jnp.bfloat16)).astype(jnp.float32)

def with_zero_row(matrix):
    return jnp.concatenate([matrix, jnp.zeros((1,) + matrix.shape[1:], matrix.dtype)], axis=0)

def key_windows(rows):
    row_count = rows.shape[0]
    leading = jnp.zeros((SPAN,) + rows.shape[1:], rows.dtype)
    earlier = jnp.concatenate([leading, rows[:row_count - SPAN]], axis=0)
    shape_out = (row_count // SPAN, SPAN) + rows.shape[1:]
    return jnp.concatenate([earlier.reshape(shape_out), rows.reshape(shape_out)], axis=1)

def fold_windows(stacked):
    current = stacked[:, SPAN:]
    earlier = stacked[:, :SPAN]
    return current + jnp.concatenate([earlier[1:], jnp.zeros_like(earlier[:1])], axis=0)

def span_probs(queries, key_rows, key_live):
    scores = jnp.einsum('qhd,khd->hqk', queries, key_rows, precision=highest) * HEAD_DIM ** (-0.5)
    itself = jnp.arange(2 * SPAN)[None, :] == jnp.arange(SPAN)[:, None] + SPAN
    scores = jnp.where(itself[None], scores - self_penalty, scores)
    scores = jnp.where(key_live[None, None, :], scores, masked_score)
    largest = lax.optimization_barrier(jnp.max(scores, axis=-1, keepdims=True))
    lifted = jnp.exp(scores - largest)
    summed = lax.optimization_barrier(jnp.sum(lifted, axis=-1, keepdims=True))
    return (lifted / summed, (largest + jnp.log(summed))[..., 0])

def owner_forward(own_qk, own_values, occupied):
    head_count = own_qk.shape[1] // HEAD_DIM
    blocks = own_qk.shape[0] // SPAN
    queries = own_qk.reshape(blocks, SPAN, head_count, HEAD_DIM)
    key_rows = key_windows(own_qk).reshape(blocks, 2 * SPAN, head_count, HEAD_DIM)
    value_rows = key_windows(own_values).reshape(blocks, 2 * SPAN, head_count, HEAD_DIM)
    live_keys = key_windows(occupied)

    def one_block(pieces):
        block_query, block_key, block_value, block_live = pieces
        probability, log_total = span_probs(block_query, block_key, block_live)
        result = jnp.einsum('hqk,khd->qhd', rounded(probability), block_value, precision=highest)
        return (rounded(result).reshape(SPAN, head_count * HEAD_DIM), log_total.T)
    outputs, log_totals = lax.map(one_block, (queries, key_rows, value_rows, live_keys))
    return (outputs.reshape(-1, head_count * HEAD_DIM), log_totals.reshape(-1, head_count))

def owner_backward(own_qk, own_values, occupied, own_grad, own_shift):
    head_count = own_qk.shape[1] // HEAD_DIM
    blocks = own_qk.shape[0] // SPAN
    queries = own_qk.reshape(blocks, SPAN, head_count, HEAD_DIM)
    key_rows = key_windows(own_qk).reshape(blocks, 2 * SPAN, head_count, HEAD_DIM)
    value_rows = key_windows(own_values).reshape(blocks, 2 * SPAN, head_count, HEAD_DIM)
    live_keys = key_windows(occupied)
    grad_rows = own_grad.reshape(blocks, SPAN, head_count, HEAD_DIM)
    shift_rows = own_shift.reshape(blocks, SPAN, head_count)

    def one_block(pieces):
        block_query, block_key, block_value, block_live, block_grad, block_shift = pieces
        probability, log_total = span_probs(block_query, block_key, block_live)
        prob_grad = jnp.einsum('qhd,khd->hqk', block_grad, block_value, precision=highest)
        score_grad = rounded(probability * (prob_grad - block_shift.T[:, :, None]))
        query_grad = jnp.einsum('hqk,khd->qhd', score_grad, block_key, precision=highest) * HEAD_DIM ** (-0.5)
        key_grad = jnp.einsum('hqk,qhd->khd', score_grad, block_query, precision=highest) * HEAD_DIM ** (-0.5)
        value_grad = jnp.einsum('hqk,qhd->khd', rounded(probability), block_grad, precision=highest)
        return (query_grad, key_grad, value_grad)
    query_grad, key_grad, value_grad = lax.map(one_block, (queries, key_rows, value_rows, live_keys, grad_rows, shift_rows))
    row_width = head_count * HEAD_DIM
    qk_rows = (query_grad + fold_windows(key_grad)).reshape(-1, row_width).astype(jnp.bfloat16)
    value_out = fold_windows(value_grad).reshape(-1, row_width).astype(jnp.bfloat16)
    return (qk_rows, value_out)

def route_round(bucket_row, capacity):
    owners = jnp.arange(N_CTX, dtype=jnp.int32)
    ordering = jnp.argsort(bucket_row, stable=True).astype(jnp.int32)
    counts = lax.optimization_barrier(jnp.sum((bucket_row[:, None] == owners[None, :]).astype(jnp.int32), axis=0))
    starts = jnp.cumsum(counts) - counts
    offsets = jnp.arange(capacity, dtype=jnp.int32)
    occupied = offsets[None, :] < counts[:, None]
    picked = jnp.minimum(starts[:, None] + offsets[None, :], TOKENS - 1).astype(jnp.int32)
    token_index = jnp.where(occupied, ordering[picked], TOKENS).astype(jnp.int32)
    return (token_index, occupied)

def reference(shared_qk, values, out_grad, out_weight, buckets):
    capacity = 2 * TOK_DEV
    padded_qk = with_zero_row(shared_qk)
    padded_values = with_zero_row(values)
    routes = [route_round(buckets[round_index], capacity) for round_index in range(ROUNDS)]
    round_outputs = []
    round_logs = []
    for round_index in range(ROUNDS):
        token_index, occupied = routes[round_index]

        def owner_step(pieces):
            owner_tokens, owner_live = pieces
            own_qk = padded_qk[owner_tokens].astype(jnp.float32)
            own_values = padded_values[owner_tokens].astype(jnp.float32)
            rows_out, logs_out = owner_forward(own_qk, own_values, owner_live)
            return (rows_out.astype(jnp.bfloat16), logs_out)
        rows_all, logs_all = lax.map(owner_step, (token_index, occupied))
        flat_index = token_index.reshape(-1)
        round_outputs.append(jnp.zeros((TOKENS + 1, D), jnp.bfloat16).at[flat_index].set(rows_all.reshape(-1, D))[:TOKENS])
        round_logs.append(jnp.zeros((TOKENS + 1, HEADS), jnp.float32).at[flat_index].set(logs_all.reshape(-1, HEADS))[:TOKENS])
    log_stack = jnp.stack(round_logs)
    largest = lax.optimization_barrier(jnp.max(log_stack, axis=0))
    lifted = jnp.exp(log_stack - largest)
    round_weight = lifted / lax.optimization_barrier(jnp.sum(lifted, axis=0))
    row_stack = jnp.stack(round_outputs).astype(jnp.float32).reshape(ROUNDS, TOKENS, HEADS, HEAD_DIM)
    attended = lax.optimization_barrier(jnp.sum(round_weight[..., None] * row_stack, axis=0)).reshape(TOKENS, D).astype(jnp.bfloat16)
    mixed = jnp.dot(attended, out_weight.T, preferred_element_type=jnp.float32).astype(jnp.bfloat16)
    attended_grad = jnp.dot(out_grad, out_weight, preferred_element_type=jnp.float32)
    grad_weight = jnp.dot(out_grad.T, attended, preferred_element_type=jnp.float32) * (1.0 / math.sqrt(TOKENS))
    grad_heads = attended_grad.reshape(TOKENS, HEADS, HEAD_DIM)
    inner = lax.optimization_barrier(jnp.sum(grad_heads * attended.astype(jnp.float32).reshape(TOKENS, HEADS, HEAD_DIM), axis=-1))
    qk_total = jnp.zeros((TOKENS, D), jnp.float32)
    value_total = jnp.zeros((TOKENS, D), jnp.float32)
    for round_index in range(ROUNDS):
        token_index, occupied = routes[round_index]
        query_grad = (round_weight[round_index][..., None] * grad_heads).reshape(TOKENS, D).astype(jnp.bfloat16)
        padded_grad = with_zero_row(query_grad)
        padded_shift = with_zero_row(round_weight[round_index] * inner)

        def owner_back(pieces):
            owner_tokens, owner_live = pieces
            own_qk = padded_qk[owner_tokens].astype(jnp.float32)
            own_values = padded_values[owner_tokens].astype(jnp.float32)
            own_grad = padded_grad[owner_tokens].astype(jnp.float32)
            own_shift = padded_shift[owner_tokens]
            return owner_backward(own_qk, own_values, owner_live, own_grad, own_shift)
        qk_all, value_all = lax.map(owner_back, (token_index, occupied))
        flat_index = token_index.reshape(-1)
        qk_total = qk_total + jnp.zeros((TOKENS + 1, D), jnp.bfloat16).at[flat_index].set(qk_all.reshape(-1, D))[:TOKENS].astype(jnp.float32)
        value_total = value_total + jnp.zeros((TOKENS + 1, D), jnp.bfloat16).at[flat_index].set(value_all.reshape(-1, D))[:TOKENS].astype(jnp.float32)
    return (mixed, qk_total.astype(jnp.bfloat16), value_total.astype(jnp.bfloat16), grad_weight)
```

```python
import math

import jax
import jax.numpy as jnp
from jax import lax
from jax.experimental import pallas as pl
from jax.experimental.pallas import tpu as pltpu
from jax.sharding import PartitionSpec as P

NX, NZ, NY = 4, 8, 4
NG = NX * NY
TOK = 128
DIM = 128
ROUNDS = 2
BUCKETS = 8
SLOTS = 256
SCALE = DIM ** (-0.5)
SELF_PENALTY = 10000.0
MASKED = -1e30
BF = jnp.bfloat16
F32 = jnp.float32


def ctx_of(x, z, y):
    return (x * NZ + z) * NY + y


RINGS = [[ctx_of(x, z, y) for z in range(NZ)] for x in range(NX) for y in range(NY)]
PLANES = [[ctx_of(x, z, y) for x in range(NX) for y in range(NY)] for z in range(NZ)]

ROW_W = 512
ROW_LIVE = 640
ROWS_B = 656
ROW_EXTRA = 256
ROWS_C = 272
ROW_GW = 512
ROWS_E = 640
ROWS_A = 288
ROWS_F = 416


def iota(shape, dim):
    return lax.broadcasted_iota(jnp.int32, shape, dim)


def fiota(shape, dim):
    return iota(shape, dim).astype(F32)


def dot(a, b):
    return jnp.dot(a, b, preferred_element_type=F32)


def dot_nt(a, b):
    return lax.dot_general(a, b, (((1,), (1,)), ((), ())), preferred_element_type=F32)


def dot_tn(a, b):
    return lax.dot_general(a, b, (((0,), (0,)), ((), ())), preferred_element_type=F32)


def ones_where(mask):
    return jnp.where(mask, 1.0, 0.0).astype(BF)


def swap_matrix():
    dest = iota((TOK, TOK), 0)
    source = ((dest >> 1) & 7) * 16 + (dest >> 4) * 2 + (dest & 1)
    return ones_where(iota((TOK, TOK), 1) == source)


def three_parts(spread, lane):
    high = spread.astype(BF).astype(F32)
    rest = spread - high
    middle = rest.astype(BF).astype(F32)
    low = rest - middle
    return jnp.where(lane < 16, high, jnp.where(lane < 32, middle, jnp.where(lane < 48, low, 0.0)))


def split_slot(slot):
    owner = jnp.floor(slot * (1.0 / 16.0))
    inside = slot - 16.0 * owner
    bucket = jnp.floor(inside * 0.5)
    return owner, bucket, inside - 2.0 * bucket


def pack_ring(qk_ref, v_ref, w_ref, b_ref, msg_ref):
    for z in range(NZ):
        cols = slice(z * DIM, (z + 1) * DIM)
        msg_ref[z, 0:128, :] = qk_ref[:, cols]
        msg_ref[z, 128:256, :] = v_ref[:, cols]
        msg_ref[z, 256:272, :] = w_ref[:, cols]
        msg_ref[z, 272:288, :] = b_ref[...]


def route(a_ref, msg_ref, srow_ref, scol_ref, y_ref):
    sub = iota((TOK, TOK), 0)
    lane = iota((TOK, TOK), 1)
    swap = swap_matrix()
    slot_sub = fiota((SLOTS, TOK), 0)
    live = jnp.zeros((SLOTS, TOK), F32)
    scols = jnp.zeros((TOK, TOK), F32)
    for r in range(ROUNDS):
        for z in range(NZ):
            brow = a_ref[z, 272:288, :].astype(F32)[r : r + 1, :]
            bcol = jnp.sum(jnp.where(sub == lane, brow, 0.0), axis=1, keepdims=True)
            same = jnp.where(bcol == brow, 1.0, 0.0)
            prow = jnp.sum(jnp.where(sub < lane, same, 0.0), axis=0, keepdims=True)
            pcol = jnp.sum(jnp.where(lane < sub, same, 0.0), axis=1, keepdims=True)
            srow = 2.0 * brow + prow
            scol = 2.0 * bcol + pcol
            srow_ref[r * NZ + z : r * NZ + z + 1, :] = srow
            scols = jnp.where(lane == r * NZ + z, scol, scols)
            rows = jnp.concatenate([a_ref[z, 0:128, :], a_ref[z, 128:256, :]], axis=1)
            y_ref[z, :, :] = dot(ones_where(slot_sub == srow), rows).astype(BF)
            owner, _, _ = split_slot(srow)
            place = owner * 16.0 + (2.0 * z) + prow
            _, bucket, _ = split_slot(scol)
            mark = ones_where(lane.astype(F32) == bucket + (1.0 * r * BUCKETS))
            live = live + dot(ones_where(slot_sub == place), mark)
        for o in range(NG):
            block = y_ref[:, o * 16 : (o + 1) * 16, :].reshape(TOK, 2 * DIM)
            moved = dot(swap, block).astype(BF)
            msg_ref[o, r * 128 : (r + 1) * 128, :] = moved[:, :DIM]
            msg_ref[o, 256 + r * 128 : 256 + (r + 1) * 128, :] = moved[:, DIM:]
    scol_ref[...] = scols
    live = live.astype(BF)
    for o in range(NG):
        msg_ref[o, ROW_LIVE:ROWS_B, :] = live[o * 16 : (o + 1) * 16, :]
        for z in range(NZ):
            msg_ref[o, ROW_W + z * 16 : ROW_W + (z + 1) * 16, :] = a_ref[z, 256:272, :]


def raw_scores(q):
    scores = dot_nt(q, q) * SCALE
    itself = iota((SLOTS, SLOTS), 0) == iota((SLOTS, SLOTS), 1)
    return jnp.where(itself, scores - SELF_PENALTY, scores)


def bucket_rows(ref, start):
    return ref[:, start : start + 16, :].reshape(SLOTS, DIM)


def attend(b_ref, msg_ref, logs_ref, qcode_ref, kcode_ref, w_ref):
    lane = iota((SLOTS, TOK), 1)
    live = bucket_rows(b_ref, ROW_LIVE)

    def order(j):
        return (j >> 6) * 64 + ((j >> 1) & 7) * 8 + ((j >> 4) & 3) * 2 + (j & 1)

    earlier = ones_where(order(iota((SLOTS, SLOTS), 1)) < order(iota((SLOTS, SLOTS), 0)))
    rank = dot(earlier, live)
    span = jnp.where(rank >= 128.0, 1.0, 0.0)
    kcol = jnp.where(live.astype(F32) > 0.5, span, 2.0).astype(BF)
    pick = ones_where(iota((16, TOK), 0) == iota((16, TOK), 1))
    krows = dot_nt(pick, kcol)
    qcode_ref[...] = span
    kcode_ref[...] = krows
    logs = jnp.zeros((SLOTS, TOK), F32)
    for r in range(ROUNDS):
        for k in range(BUCKETS):
            n = r * BUCKETS + k
            q = bucket_rows(b_ref, r * 128 + k * 16)
            v = bucket_rows(b_ref, 256 + r * 128 + k * 16)
            scores = jnp.where(krows[n : n + 1, :] <= span[:, n : n + 1], raw_scores(q), MASKED)
            largest = jnp.max(scores, axis=1, keepdims=True)
            lifted = jnp.exp(scores - largest)
            summed = jnp.sum(lifted, axis=1, keepdims=True)
            probability = (lifted * (1.0 / summed)).astype(BF)
            out = dot(probability, v).astype(BF)
            msg_ref[:, r * 128 + k * 16 : r * 128 + (k + 1) * 16, :] = out.reshape(NG, 16, DIM)
            logs = jnp.where((lane & 15) == n, largest + jnp.log(summed), logs)
    logs_ref[...] = logs
    msg_ref[:, ROW_EXTRA:ROWS_C, :] = three_parts(logs, lane).astype(BF).reshape(NG, 16, DIM)
    for x in range(NX):
        for y in range(NY):
            for z in range(NZ):
                at = ctx_of(x, z, y) * 16
                w_ref[at : at + 16, :] = b_ref[x * NY + y, ROW_W + z * 16 : ROW_W + (z + 1) * 16, :]


def combine(c_ref, srow_ref, scol_ref, grad_ref, msg_ref, att_ref, y_ref, s_ref):
    lane = iota((TOK, TOK), 1)
    swap = swap_matrix()
    slot_sub = fiota((SLOTS, TOK), 0)
    slot_lane = fiota((TOK, SLOTS), 1)
    for r in range(ROUNDS):
        for o in range(NG):
            moved = dot(swap, c_ref[o, r * 128 : (r + 1) * 128, :]).astype(BF)
            y_ref[r, :, o * 16 : (o + 1) * 16, :] = moved.reshape(NZ, 16, DIM)
    log_rows = bucket_rows(c_ref, ROW_EXTRA)
    extra = jnp.zeros((SLOTS, TOK), F32)
    folded = lane & 15
    for z in range(NZ):
        outs, logs, marks = [], [], []
        for r in range(ROUNDS):
            n = r * NZ + z
            scol = scol_ref[:, n : n + 1]
            outs.append(dot(ones_where(slot_lane == scol), y_ref[r, z]))
            owner, bucket, place = split_slot(scol)
            parts = dot(ones_where(slot_lane == owner * 16.0 + (2.0 * z) + place), log_rows)
            mark = folded.astype(F32) == bucket + (1.0 * r * BUCKETS)
            marks.append(mark)
            logs.append(jnp.sum(jnp.where(mark, parts, 0.0), axis=1, keepdims=True))
        largest = jnp.maximum(logs[0], logs[1])
        lifted = [jnp.exp(log - largest) for log in logs]
        total = lifted[0] + lifted[1]
        weights = [one / total for one in lifted]
        att = (weights[0] * outs[0] + weights[1] * outs[1]).astype(BF)
        att_ref[z * TOK : (z + 1) * TOK, :] = att
        grad = grad_ref[z * TOK : (z + 1) * TOK, :]
        inner = jnp.sum(grad * att.astype(F32), axis=1, keepdims=True)
        for r in range(ROUNDS):
            n = r * NZ + z
            srow = srow_ref[n : n + 1, :]
            query_grad = (weights[r] * grad).astype(BF)
            s_ref[r, z] = dot(ones_where(slot_sub == srow), query_grad).astype(BF)
            owner, _, place = split_slot(srow)
            spread = jnp.where(marks[r], weights[r] * inner, 0.0)
            extra = extra + dot(
                ones_where(slot_sub == owner * 16.0 + (2.0 * z) + place),
                three_parts(spread, lane).astype(BF),
            )
    for r in range(ROUNDS):
        for o in range(NG):
            block = s_ref[r, :, o * 16 : (o + 1) * 16, :].reshape(TOK, DIM)
            msg_ref[o, r * 128 : (r + 1) * 128, :] = dot(swap, block).astype(BF)
    msg_ref[:, ROW_EXTRA:ROWS_C, :] = extra.astype(BF).reshape(NG, 16, DIM)


def attend_back(b_ref, d_ref, logs_ref, qcode_ref, kcode_ref, gw_ref, msg_ref):
    lane = iota((SLOTS, TOK), 1)
    shifts = bucket_rows(d_ref, ROW_EXTRA).astype(F32)
    for r in range(ROUNDS):
        for k in range(BUCKETS):
            n = r * BUCKETS + k
            q = bucket_rows(b_ref, r * 128 + k * 16)
            v = bucket_rows(b_ref, 256 + r * 128 + k * 16)
            g = bucket_rows(d_ref, r * 128 + k * 16)
            shift = jnp.sum(jnp.where((lane & 15) == n, shifts, 0.0), axis=1, keepdims=True)
            seen = kcode_ref[n : n + 1, :] <= qcode_ref[:, n : n + 1]
            scores = jnp.where(seen, raw_scores(q), MASKED)
            probability = jnp.exp(scores - logs_ref[:, n : n + 1])
            score_grad = (probability * (dot_nt(g, v) - shift)).astype(BF)
            qk_grad = (dot(score_grad, q) + dot_tn(score_grad, q)) * SCALE
            value_grad = dot_tn(probability.astype(BF), g)
            rows = slice(r * 128 + k * 16, r * 128 + (k + 1) * 16)
            msg_ref[:, rows, :] = qk_grad.astype(BF).reshape(NG, 16, DIM)
            rows = slice(256 + r * 128 + k * 16, 256 + r * 128 + (k + 1) * 16)
            msg_ref[:, rows, :] = value_grad.astype(BF).reshape(NG, 16, DIM)
    for x in range(NX):
        for y in range(NY):
            for z in range(NZ):
                at = ctx_of(x, z, y) * 16
                msg_ref[x * NY + y, ROW_GW + z * 16 : ROW_GW + (z + 1) * 16, :] = gw_ref[at : at + 16, :]


def gather_home(e_ref, scol_ref, att_ref, msg_ref, y_ref):
    swap = swap_matrix()
    slot_lane = fiota((TOK, SLOTS), 1)
    for r in range(ROUNDS):
        for o in range(NG):
            rows = jnp.concatenate(
                [
                    e_ref[o, r * 128 : (r + 1) * 128, :],
                    e_ref[o, 256 + r * 128 : 256 + (r + 1) * 128, :],
                ],
                axis=1,
            )
            y_ref[r, :, o * 16 : (o + 1) * 16, :] = dot(swap, rows).astype(BF).reshape(NZ, 16, 2 * DIM)
    total = jnp.zeros((TOK, DIM), F32)
    for o in range(NG):
        total = total + e_ref[o, ROW_GW:ROWS_E, :].astype(F32)
    total = total * (1.0 / math.sqrt(NX * NY * NZ * TOK))
    high = total.astype(BF)
    low = (total - high.astype(F32)).astype(BF)
    for z in range(NZ):
        rows = jnp.zeros((TOK, 2 * DIM), F32)
        for r in range(ROUNDS):
            n = r * NZ + z
            rows = rows + dot(ones_where(slot_lane == scol_ref[:, n : n + 1]), y_ref[r, z])
        rows = rows.astype(BF)
        msg_ref[z, 0:128, :] = rows[:, :DIM]
        msg_ref[z, 128:256, :] = rows[:, DIM:]
        msg_ref[z, 256:384, :] = att_ref[z * TOK : (z + 1) * TOK, :]
        msg_ref[z, 384:400, :] = high[z * 16 : (z + 1) * 16, :]
        msg_ref[z, 400:416, :] = low[z * 16 : (z + 1) * 16, :]


def unpack_ring(f_ref, qk_ref, v_ref, att_ref, gw_ref):
    for z in range(NZ):
        cols = slice(z * DIM, (z + 1) * DIM)
        qk_ref[:, cols] = f_ref[z, 0:128, :]
        v_ref[:, cols] = f_ref[z, 128:256, :]
        att_ref[:, cols] = f_ref[z, 256:384, :]
        gw_ref[:, cols] = f_ref[z, 384:400, :].astype(F32) + f_ref[z, 400:416, :].astype(F32)


def on_device(body, outs, scratch=()):
    shapes = [jax.ShapeDtypeStruct(shape, kind) for shape, kind in outs]

    def call(*operands):
        return pl.pallas_call(
            body,
            out_shape=shapes,
            in_specs=[pl.BlockSpec(memory_space=pltpu.VMEM)] * len(operands),
            out_specs=[pl.BlockSpec(memory_space=pltpu.VMEM)] * len(shapes),
            scratch_shapes=[pltpu.VMEM(shape, kind) for shape, kind in scratch],
            compiler_params=pltpu.CompilerParams(vmem_limit_bytes=40 * 1024 * 1024),
        )(*operands)

    return call


def exchange(message, groups):
    return lax.all_to_all(
        message, "ctx", split_axis=0, concat_axis=0, tiled=True, axis_index_groups=groups
    )


def per_device(shared_qk, values, out_grad, out_weight, buckets):
    core = lax.axis_index("head")
    width = shared_qk.shape[1]
    ring_grad = lax.all_gather(out_grad, "ctx", axis=0, tiled=True, axis_index_groups=RINGS)
    whole_weight = lax.all_gather(out_weight, "ctx", axis=0, tiled=True)
    other_grad = lax.ppermute(ring_grad, "head", [(0, 1), (1, 0)])

    bucket_tile = jnp.pad(buckets.astype(BF), ((0, 14), (0, 0)))
    (msg,) = on_device(pack_ring, [((NZ, ROWS_A, DIM), BF)])(
        shared_qk, values, out_weight, bucket_tile
    )
    got_a = exchange(msg, RINGS)
    msg, slot_rows, slot_cols = on_device(
        route,
        [((NG, ROWS_B, DIM), BF), ((16, TOK), F32), ((TOK, TOK), F32)],
        [((NZ, SLOTS, 2 * DIM), BF)],
    )(got_a)
    got_b = exchange(msg, PLANES)
    msg, logs, query_code, key_code, head_weight = on_device(
        attend,
        [
            ((NG, ROWS_C, DIM), BF),
            ((SLOTS, TOK), F32),
            ((SLOTS, TOK), F32),
            ((16, SLOTS), F32),
            ((2 * width, DIM), BF),
        ],
    )(got_b)
    got_c = exchange(msg, PLANES)
    own_part = lax.dynamic_slice_in_dim(head_weight, core * width, width, 0)
    other_part = lax.dynamic_slice_in_dim(head_weight, (1 - core) * width, width, 0)
    attended_grad = dot(ring_grad, own_part) + dot(other_grad, other_part)
    msg, attended = on_device(
        combine,
        [((NG, ROWS_C, DIM), BF), ((NZ * TOK, DIM), BF)],
        [((ROUNDS, NZ, SLOTS, DIM), BF), ((ROUNDS, NZ, SLOTS, DIM), BF)],
    )(got_c, slot_rows, slot_cols, attended_grad)
    got_d = exchange(msg, PLANES)
    own_gw = dot_tn(ring_grad, attended).astype(BF)
    other_gw = dot_tn(other_grad, attended).astype(BF)
    both_gw = jnp.concatenate(
        [jnp.where(core == 0, own_gw, other_gw), jnp.where(core == 0, other_gw, own_gw)], axis=0
    )
    (msg,) = on_device(attend_back, [((NG, ROWS_E, DIM), BF)])(
        got_b, got_d, logs, query_code, key_code, both_gw
    )
    got_e = exchange(msg, PLANES)
    (msg,) = on_device(
        gather_home, [((NZ, ROWS_F, DIM), BF)], [((ROUNDS, NZ, SLOTS, 2 * DIM), BF)]
    )(got_e, slot_cols, attended)
    got_f = exchange(msg, RINGS)
    grad_qk, grad_values, attended_rows, grad_weight = on_device(
        unpack_ring,
        [((TOK, width), BF), ((TOK, width), BF), ((TOK, width), BF), ((16, width), F32)],
    )(got_f)
    partial_rows = dot_nt(attended_rows, whole_weight)
    mine = lax.dynamic_slice_in_dim(partial_rows, core * width, width, 1)
    theirs = lax.dynamic_slice_in_dim(partial_rows, (1 - core) * width, width, 1)
    mixed = (mine + lax.ppermute(theirs, "head", [(0, 1), (1, 0)])).astype(BF)
    return (mixed, grad_qk, grad_values, grad_weight)


def solution(mesh):
    assert mesh.shape["ctx"] == NX * NY * NZ and mesh.shape["head"] == 2
    in_specs = (
        P("ctx", "head"),
        P("ctx", "head"),
        P("ctx", "head"),
        P("ctx", "head"),
        P(None, "ctx"),
    )
    out_specs = (P("ctx", "head"), P("ctx", "head"), P("ctx", "head"), P("ctx", "head"))
    return jax.shard_map(
        per_device, mesh=mesh, in_specs=in_specs, out_specs=out_specs, check_vma=False
    )
```

```python
import math

import jax
import jax.numpy as jnp
from jax import lax
from jax.experimental import pallas as pl
from jax.experimental.pallas import tpu as pltpu
from jax.sharding import PartitionSpec as P

NX, NZ, NY = 4, 8, 4
NG = NX * NY
TOK = 128
DIM = 128
ROUNDS = 2
BUCKETS = 8
SLOTS = 256
SCALE = DIM ** (-0.5)
SELF_PENALTY = 10000.0
MASKED = -1e30
BF = jnp.bfloat16
F32 = jnp.float32


def ctx_of(x, z, y):
    return (x * NZ + z) * NY + y


RINGS = [[ctx_of(x, z, y) for z in range(NZ)] for x in range(NX) for y in range(NY)]
PLANES = [[ctx_of(x, z, y) for x in range(NX) for y in range(NY)] for z in range(NZ)]

ROW_W = 512
ROW_LIVE = 640
ROWS_B = 656
ROW_EXTRA = 256
ROWS_C = 272
ROW_PLANE = 272
ROWS_D = 400
ROW_GW = 512
ROWS_E = 640
ROWS_A = 288
ROWS_F = 416


def iota(shape, dim):
    return lax.broadcasted_iota(jnp.int32, shape, dim)


def fiota(shape, dim):
    return iota(shape, dim).astype(F32)


def dot(a, b):
    return jnp.dot(a, b, preferred_element_type=F32)


def dot_nt(a, b):
    return lax.dot_general(a, b, (((1,), (1,)), ((), ())), preferred_element_type=F32)


def dot_tn(a, b):
    return lax.dot_general(a, b, (((0,), (0,)), ((), ())), preferred_element_type=F32)


def ones_where(mask):
    return jnp.where(mask, 1.0, 0.0).astype(BF)


def swap_matrix():
    dest = iota((TOK, TOK), 0)
    source = ((dest >> 1) & 7) * 16 + (dest >> 4) * 2 + (dest & 1)
    return ones_where(iota((TOK, TOK), 1) == source)


def three_parts(spread, lane):
    high = spread.astype(BF).astype(F32)
    rest = spread - high
    middle = rest.astype(BF).astype(F32)
    low = rest - middle
    return jnp.where(lane < 16, high, jnp.where(lane < 32, middle, jnp.where(lane < 48, low, 0.0)))


def split_slot(slot):
    owner = jnp.floor(slot * (1.0 / 16.0))
    inside = slot - 16.0 * owner
    bucket = jnp.floor(inside * 0.5)
    return owner, bucket, inside - 2.0 * bucket


def pack_ring(qk_ref, v_ref, w_ref, b_ref, msg_ref, sems):
    copies = []
    for z in range(NZ):
        cols = slice(z * DIM, (z + 1) * DIM)
        for i, (ref, start, rows) in enumerate(((qk_ref, 0, 128), (v_ref, 128, 128), (w_ref, 256, 16))):
            copies.append(
                pltpu.make_async_copy(ref.at[:, cols], msg_ref.at[z, start : start + rows, :], sems.at[z, i])
            )
            copies[-1].start()
    rows = jnp.concatenate([b_ref[...].astype(F32), jnp.zeros((14, TOK), F32)], axis=0).astype(BF)
    for z in range(NZ):
        msg_ref[z, 272:288, :] = rows
    for copy in copies:
        copy.wait()


def route(a_ref, msg_ref, slot_ref, y_ref):
    sub = iota((TOK, TOK), 0)
    lane = iota((TOK, TOK), 1)
    swap = swap_matrix()
    slot_sub = fiota((SLOTS, TOK), 0)
    live = jnp.zeros((SLOTS, TOK), F32)
    scols = jnp.zeros((TOK, TOK), F32)
    for r in range(ROUNDS):
        for z in range(NZ):
            brow = a_ref[z, 272:288, :].astype(F32)[r : r + 1, :]
            bcol = jnp.sum(jnp.where(sub == lane, brow, 0.0), axis=1, keepdims=True)
            same = jnp.where(bcol == brow, 1.0, 0.0)
            prow = jnp.sum(jnp.where(sub < lane, same, 0.0), axis=0, keepdims=True)
            pcol = jnp.sum(jnp.where(lane < sub, same, 0.0), axis=1, keepdims=True)
            srow = 2.0 * brow + prow
            scol = 2.0 * bcol + pcol
            slot_ref[r * NZ + z : r * NZ + z + 1, :] = srow
            scols = jnp.where(lane == r * NZ + z, scol, scols)
            rows = jnp.concatenate([a_ref[z, 0:128, :], a_ref[z, 128:256, :]], axis=1)
            y_ref[z, :, :] = dot(ones_where(slot_sub == srow), rows).astype(BF)
            owner, _, _ = split_slot(srow)
            place = owner * 16.0 + (2.0 * z) + prow
            _, bucket, _ = split_slot(scol)
            mark = ones_where(lane.astype(F32) == bucket + (1.0 * r * BUCKETS))
            live = live + dot(ones_where(slot_sub == place), mark)
        for o in range(NG):
            block = y_ref[:, o * 16 : (o + 1) * 16, :].reshape(TOK, 2 * DIM)
            moved = dot(swap, block).astype(BF)
            msg_ref[o, r * 128 : (r + 1) * 128, :] = moved[:, :DIM]
            msg_ref[o, 256 + r * 128 : 256 + (r + 1) * 128, :] = moved[:, DIM:]
    slot_ref[16:144, :] = scols
    live = live.astype(BF)
    for o in range(NG):
        msg_ref[o, ROW_LIVE:ROWS_B, :] = live[o * 16 : (o + 1) * 16, :]
        for z in range(NZ):
            msg_ref[o, ROW_W + z * 16 : ROW_W + (z + 1) * 16, :] = a_ref[z, 256:272, :]


def raw_scores(q):
    scores = dot_nt(q, q) * SCALE
    itself = iota((SLOTS, SLOTS), 0) == iota((SLOTS, SLOTS), 1)
    return jnp.where(itself, scores - SELF_PENALTY, scores)


def bucket_rows(ref, start):
    return ref[:, start : start + 16, :].reshape(SLOTS, DIM)


def attend(b_ref, msg_ref, state_ref, w_ref):
    lane = iota((SLOTS, TOK), 1)
    live = bucket_rows(b_ref, ROW_LIVE)

    def order(j):
        return (j >> 6) * 64 + ((j >> 1) & 7) * 8 + ((j >> 4) & 3) * 2 + (j & 1)

    earlier = ones_where(order(iota((SLOTS, SLOTS), 1)) < order(iota((SLOTS, SLOTS), 0)))
    rank = dot(earlier, live)
    span = jnp.where(rank >= 128.0, 1.0, 0.0)
    kcol = jnp.where(live.astype(F32) > 0.5, span, 2.0).astype(BF)
    pick = ones_where(iota((16, TOK), 0) == iota((16, TOK), 1))
    krows = dot_nt(pick, kcol)
    logs = jnp.zeros((SLOTS, TOK), F32)
    for r in range(ROUNDS):
        for k in range(BUCKETS):
            n = r * BUCKETS + k
            q = bucket_rows(b_ref, r * 128 + k * 16)
            v = bucket_rows(b_ref, 256 + r * 128 + k * 16)
            scores = jnp.where(krows[n : n + 1, :] <= span[:, n : n + 1], raw_scores(q), MASKED)
            largest = jnp.max(scores, axis=1, keepdims=True)
            lifted = jnp.exp(scores - largest)
            summed = jnp.sum(lifted, axis=1, keepdims=True)
            probability = (lifted * (1.0 / summed)).astype(BF)
            out = dot(probability, v).astype(BF)
            msg_ref[:, r * 128 + k * 16 : r * 128 + (k + 1) * 16, :] = out.reshape(NG, 16, DIM)
            logs = jnp.where((lane & 15) == n, largest + jnp.log(summed), logs)
    shifted = dot_nt(span.astype(BF), ones_where(iota((TOK, TOK), 0) == iota((TOK, TOK), 1) + 16))
    state_ref[0:256, :] = jnp.where(lane < 16, logs, shifted)
    state_ref[256:272, :] = krows[:, 0:128]
    state_ref[272:288, :] = krows[:, 128:256]
    msg_ref[:, ROW_EXTRA:ROWS_C, :] = three_parts(logs, lane).astype(BF).reshape(NG, 16, DIM)
    for x in range(NX):
        for y in range(NY):
            for z in range(NZ):
                at = ctx_of(x, z, y) * 16
                w_ref[at : at + 16, :] = b_ref[x * NY + y, ROW_W + z * 16 : ROW_W + (z + 1) * 16, :]


def combine(z_ref, c_ref, slot_ref, grad_ref, weight_ref, msg_ref, att_ref, turned_ref, y_ref, s_ref):
    lane = iota((TOK, TOK), 1)
    swap = swap_matrix()
    slot_sub = fiota((SLOTS, TOK), 0)
    slot_lane = fiota((TOK, SLOTS), 1)
    for r in range(ROUNDS):
        for o in range(NG):
            moved = dot(swap, c_ref[o, r * 128 : (r + 1) * 128, :]).astype(BF)
            y_ref[r, :, o * 16 : (o + 1) * 16, :] = moved.reshape(NZ, 16, DIM)
    log_rows = bucket_rows(c_ref, ROW_EXTRA)
    extra = jnp.zeros((SLOTS, TOK), F32)
    folded = lane & 15
    for z in range(NZ):
        outs, logs, marks = [], [], []
        for r in range(ROUNDS):
            n = r * NZ + z
            scol = slot_ref[16:144, n : n + 1]
            outs.append(dot(ones_where(slot_lane == scol), y_ref[r, z]))
            owner, bucket, place = split_slot(scol)
            parts = dot(ones_where(slot_lane == owner * 16.0 + (2.0 * z) + place), log_rows)
            mark = folded.astype(F32) == bucket + (1.0 * r * BUCKETS)
            marks.append(mark)
            logs.append(jnp.sum(jnp.where(mark, parts, 0.0), axis=1, keepdims=True))
        largest = jnp.maximum(logs[0], logs[1])
        lifted = [jnp.exp(log - largest) for log in logs]
        total = lifted[0] + lifted[1]
        weights = [one / total for one in lifted]
        att = (weights[0] * outs[0] + weights[1] * outs[1]).astype(BF)
        att_ref[z * TOK : (z + 1) * TOK, :] = att
        turned = pl.ds(pl.multiple_of(lax.rem(z_ref[0] - z + NZ, NZ) * TOK, TOK), TOK)
        turned_ref[turned, :] = att
        grad = grad_ref[turned, :]
        inner = jnp.sum(grad * att.astype(F32), axis=1, keepdims=True)
        for r in range(ROUNDS):
            n = r * NZ + z
            srow = slot_ref[n : n + 1, :]
            query_grad = (weights[r] * grad).astype(BF)
            s_ref[r, z] = dot(ones_where(slot_sub == srow), query_grad).astype(BF)
            owner, _, place = split_slot(srow)
            spread = jnp.where(marks[r], weights[r] * inner, 0.0)
            extra = extra + dot(
                ones_where(slot_sub == owner * 16.0 + (2.0 * z) + place),
                three_parts(spread, lane).astype(BF),
            )
    for r in range(ROUNDS):
        for o in range(NG):
            block = s_ref[r, :, o * 16 : (o + 1) * 16, :].reshape(TOK, DIM)
            msg_ref[o, r * 128 : (r + 1) * 128, :] = dot(swap, block).astype(BF)
    msg_ref[:, ROW_EXTRA:ROWS_C, :] = extra.astype(BF).reshape(NG, 16, DIM)
    for h in range(NZ):
        part = weight_ref[:, h * DIM : (h + 1) * DIM]
        for o in range(NG):
            msg_ref[o, ROW_PLANE + h * 16 : ROW_PLANE + (h + 1) * 16, :] = part


def attend_back(b_ref, d_ref, state_ref, gw_ref, msg_ref, mark_ref):
    lane = iota((SLOTS, TOK), 1)
    shifts = bucket_rows(d_ref, ROW_EXTRA).astype(F32)
    krows = jnp.concatenate([state_ref[256:272, :], state_ref[272:288, :]], axis=1)
    mark_ref[...] = krows[0:8, 0:128]
    for r in range(ROUNDS):
        for k in range(BUCKETS):
            n = r * BUCKETS + k
            q = bucket_rows(b_ref, r * 128 + k * 16)
            v = bucket_rows(b_ref, 256 + r * 128 + k * 16)
            g = bucket_rows(d_ref, r * 128 + k * 16)
            shift = jnp.sum(jnp.where((lane & 15) == n, shifts, 0.0), axis=1, keepdims=True)
            seen = krows[n : n + 1, :] <= state_ref[0:256, 16 + n : 17 + n]
            scores = jnp.where(seen, raw_scores(q), MASKED)
            probability = jnp.exp(scores - state_ref[0:256, n : n + 1])
            score_grad = (probability * (dot_nt(g, v) - shift)).astype(BF)
            qk_grad = (dot(score_grad, q) + dot_tn(score_grad, q)) * SCALE
            value_grad = dot_tn(probability.astype(BF), g)
            rows = slice(r * 128 + k * 16, r * 128 + (k + 1) * 16)
            msg_ref[:, rows, :] = qk_grad.astype(BF).reshape(NG, 16, DIM)
            rows = slice(256 + r * 128 + k * 16, 256 + r * 128 + (k + 1) * 16)
            msg_ref[:, rows, :] = value_grad.astype(BF).reshape(NG, 16, DIM)
    for x in range(NX):
        for y in range(NY):
            for z in range(NZ):
                at = ctx_of(x, z, y) * 16
                msg_ref[x * NY + y, ROW_GW + z * 16 : ROW_GW + (z + 1) * 16, :] = gw_ref[at : at + 16, :]


def join(*refs):
    out_ref, sems = refs[NZ:]
    copies = [
        pltpu.make_async_copy(ref, out_ref.at[n * TOK : (n + 1) * TOK, :], sems.at[n])
        for n, ref in enumerate(refs[:NZ])
    ]
    for copy in copies:
        copy.start()
    for copy in copies:
        copy.wait()


def project(place_ref, d_ref, *refs):
    own_out, other_out, plane_ref, sem = refs[NZ:]
    fetch = pltpu.make_async_copy(d_ref.at[:, ROW_PLANE:ROWS_D, :], plane_ref, sem)
    fetch.start()
    fetch.wait()
    weights = []
    for core in (place_ref[0], 1 - place_ref[0]):
        parts = []
        for turn in range(NZ):
            head = lax.rem(place_ref[1] - turn + NZ, NZ)
            rows = pl.ds(pl.multiple_of(head * 16, 16), 16)
            parts.append(plane_ref[pl.ds(core * (NG // 2), NG // 2), rows, :].reshape(NG * 8, DIM))
        weights.append(jnp.concatenate(parts, axis=1))
    weights = jnp.concatenate(weights, axis=0)
    for z in range(NZ):
        tokens = slice(z * TOK, (z + 1) * TOK)
        rows = jnp.concatenate([ref[tokens, :] for ref in refs[:NZ]], axis=1)
        both = dot_nt(rows, weights)
        own_out[tokens, :] = both[:, :DIM]
        other_out[tokens, :] = both[:, DIM:]


def gather_home(e_ref, slot_ref, own_ref, other_ref, msg_ref, y_ref):
    swap = swap_matrix()
    slot_lane = fiota((TOK, SLOTS), 1)
    for r in range(ROUNDS):
        for o in range(NG):
            rows = jnp.concatenate(
                [
                    e_ref[o, r * 128 : (r + 1) * 128, :],
                    e_ref[o, 256 + r * 128 : 256 + (r + 1) * 128, :],
                ],
                axis=1,
            )
            y_ref[r, :, o * 16 : (o + 1) * 16, :] = dot(swap, rows).astype(BF).reshape(NZ, 16, 2 * DIM)
    total = jnp.zeros((TOK, DIM), F32)
    for o in range(NG):
        total = total + e_ref[o, ROW_GW:ROWS_E, :].astype(F32)
    total = total * (1.0 / math.sqrt(NX * NY * NZ * TOK))
    high = total.astype(BF)
    low = (total - high.astype(F32)).astype(BF)
    for z in range(NZ):
        rows = jnp.zeros((TOK, 2 * DIM), F32)
        for r in range(ROUNDS):
            n = r * NZ + z
            rows = rows + dot(ones_where(slot_lane == slot_ref[16:144, n : n + 1]), y_ref[r, z])
        rows = rows.astype(BF)
        msg_ref[z, 0:128, :] = rows[:, :DIM]
        msg_ref[z, 128:256, :] = rows[:, DIM:]
        tokens = slice(z * TOK, (z + 1) * TOK)
        msg_ref[z, 256:384, :] = (own_ref[tokens, :] + other_ref[tokens, :]).astype(BF)
        msg_ref[z, 384:400, :] = high[z * 16 : (z + 1) * 16, :]
        msg_ref[z, 400:416, :] = low[z * 16 : (z + 1) * 16, :]


def unpack_ring(f_ref, qk_ref, v_ref, mixed_ref, gw_ref):
    for z in range(NZ):
        cols = slice(z * DIM, (z + 1) * DIM)
        qk_ref[:, cols] = f_ref[z, 0:128, :]
        v_ref[:, cols] = f_ref[z, 128:256, :]
        gw_ref[:, cols] = f_ref[z, 384:400, :].astype(F32) + f_ref[z, 400:416, :].astype(F32)
    for z in range(0, NZ, 2):
        first, second = f_ref[z, 256:384, :], f_ref[z + 1, 256:384, :]
        for half in range(2):
            cols = slice(half * 512 + z * 64, half * 512 + z * 64 + 128)
            part = slice(half * 64, half * 64 + 64)
            mixed_ref[:, cols] = jnp.concatenate([first[:, part], second[:, part]], axis=1)


def on_device(body, outs, scratch=(), scalars=0, hbm_in=0, hbm_out=0, vmem=24):
    shapes = [
        pltpu.HBM(shape, kind) if n < hbm_out else jax.ShapeDtypeStruct(shape, kind)
        for n, (shape, kind) in enumerate(outs)
    ]
    scratches = [pltpu.VMEM(*one) if isinstance(one, tuple) else one for one in scratch]

    def call(*operands):
        places = [pltpu.SMEM] * scalars + [pltpu.HBM] * hbm_in
        places += [pltpu.VMEM] * (len(operands) - len(places))
        return pl.pallas_call(
            body,
            out_shape=shapes,
            in_specs=[pl.BlockSpec(memory_space=place) for place in places],
            out_specs=[
                pl.BlockSpec(memory_space=pltpu.HBM if n < hbm_out else pltpu.VMEM) for n in range(len(shapes))
            ],
            scratch_shapes=scratches,
            compiler_params=pltpu.CompilerParams(vmem_limit_bytes=vmem * 1024 * 1024),
        )(*operands)

    return call


def exchange(message, groups):
    return lax.all_to_all(
        message, "ctx", split_axis=0, concat_axis=0, tiled=True, axis_index_groups=groups
    )


def swap_cores(array):
    return lax.ppermute(array, "head", [(0, 1), (1, 0)])


def pass_on(block, step):
    turn = [
        (ctx_of(x, z, y), ctx_of(x, (z + step) % NZ, y)) for x in range(NX) for z in range(NZ) for y in range(NY)
    ]
    return lax.ppermute(block, "ctx", turn)


def ring_round(forward, backward):
    return pass_on(forward, 1), pass_on(backward, -1)


def after(arrays, event):
    return lax.optimization_barrier((*arrays, event))[: len(arrays)]


def per_device(shared_qk, values, out_grad, out_weight, buckets):
    core = lax.axis_index("head")
    z_place = lax.rem(lax.axis_index("ctx") // NY, NZ)
    width = shared_qk.shape[1]

    (msg,) = on_device(
        pack_ring, [((NZ, ROWS_A, DIM), BF)], [pltpu.SemaphoreType.DMA((NZ, 3))], hbm_in=3, vmem=56
    )(shared_qk, values, out_weight, buckets)
    got_a = exchange(msg, RINGS)
    msg, slots = on_device(
        route,
        [((NG, ROWS_B, DIM), BF), ((16 + TOK, TOK), F32)],
        [((NZ, SLOTS, 2 * DIM), BF)],
    )(got_a)
    late_grad, msg = lax.optimization_barrier((out_grad, msg))
    got_b = exchange(msg, PLANES)
    before1, after1 = ring_round(late_grad, late_grad)
    before2, after2 = ring_round(before1, after1)
    before3, after3 = ring_round(before2, after2)
    before4 = pass_on(before3, 1)
    blocks = [late_grad, before1, before2, before3, before4, after3, after2, after1]
    (ring_grad,) = on_device(
        join, [((NZ * TOK, width), BF)], [pltpu.SemaphoreType.DMA((NZ,))], hbm_in=NZ, hbm_out=1
    )(*blocks)
    msg, state, head_weight = on_device(
        attend, [((NG, ROWS_C, DIM), BF), ((SLOTS + 32, TOK), F32), ((2 * width, DIM), BF)]
    )(got_b)
    got_c = exchange(msg, PLANES)
    other_grad = swap_cores(ring_grad)
    own_part = lax.dynamic_slice_in_dim(head_weight, core * width, width, 0)
    other_part = lax.dynamic_slice_in_dim(head_weight, (1 - core) * width, width, 0)
    attended_grad = dot(ring_grad, own_part) + dot(other_grad, other_part)
    msg, attended, turned = on_device(
        combine,
        [((NG, ROWS_D, DIM), BF), ((NZ * TOK, DIM), BF), ((NZ * TOK, DIM), BF)],
        [((ROUNDS, NZ, SLOTS, DIM), BF), ((ROUNDS, NZ, SLOTS, DIM), BF)],
        scalars=1,
    )(z_place.reshape(1), got_c, slots, attended_grad, out_weight)
    got_d = exchange(msg, PLANES)
    att_before1, att_after1 = ring_round(attended, attended)
    att_before2, att_after2 = ring_round(att_before1, att_after1)
    own_gw = dot_tn(ring_grad, turned).astype(BF)
    other_gw = dot_tn(other_grad, turned).astype(BF)
    both_gw = jnp.concatenate(
        [jnp.where(core == 0, own_gw, other_gw), jnp.where(core == 0, other_gw, own_gw)], axis=0
    )
    got_d, att_before2, att_after2 = lax.optimization_barrier((got_d, att_before2, att_after2))
    msg, mark = on_device(attend_back, [((NG, ROWS_E, DIM), BF), ((8, TOK), F32)])(
        got_b, got_d, state, both_gw
    )
    got_e = exchange(msg, PLANES)
    late_before2, late_after2 = after((att_before2, att_after2), mark)
    att_before3, att_after3 = ring_round(late_before2, late_after2)
    att_before4 = pass_on(att_before3, 1)
    all_attended = [attended, att_before1, att_before2, att_before3, att_before4]
    all_attended += [att_after3, att_after2, att_after1]
    own_rows, other_rows = on_device(
        project,
        [((NZ * TOK, DIM), F32), ((NZ * TOK, DIM), F32)],
        [((NG, ROWS_D - ROW_PLANE, DIM), BF), pltpu.SemaphoreType.DMA],
        scalars=1,
        hbm_in=1,
    )(jnp.stack([core, z_place]), got_d, *all_attended)
    other_rows = swap_cores(other_rows)
    (msg,) = on_device(
        gather_home, [((NZ, ROWS_F, DIM), BF)], [((ROUNDS, NZ, SLOTS, 2 * DIM), BF)]
    )(got_e, slots, own_rows, other_rows)
    got_f = exchange(msg, RINGS)
    grad_qk, grad_values, mixed, grad_weight = on_device(
        unpack_ring,
        [((TOK, width), BF), ((TOK, width), BF), ((TOK, width), BF), ((16, width), F32)],
    )(got_f)
    return (mixed, grad_qk, grad_values, grad_weight)


def solution(mesh):
    assert mesh.shape["ctx"] == NX * NY * NZ and mesh.shape["head"] == 2
    in_specs = (
        P("ctx", "head"),
        P("ctx", "head"),
        P("ctx", "head"),
        P("ctx", "head"),
        P(None, "ctx"),
    )
    out_specs = (P("ctx", "head"), P("ctx", "head"), P("ctx", "head"), P("ctx", "head"))
    return jax.shard_map(
        per_device, mesh=mesh, in_specs=in_specs, out_specs=out_specs, check_vma=False
    )
```

```python
import math

import jax
import jax.numpy as jnp
from jax import lax
from jax.experimental import pallas as pl
from jax.experimental.pallas import tpu as pltpu
from jax.sharding import PartitionSpec as P

NX, NZ, NY = 4, 8, 4
NG = NX * NY
TOK = 128
DIM = 128
ROUNDS = 2
BUCKETS = 8
SLOTS = 256
SCALE = DIM ** (-0.5)
SELF_PENALTY = 10000.0
MASKED = -1e30
BF = jnp.bfloat16
F32 = jnp.float32


def ctx_of(x, z, y):
    return (x * NZ + z) * NY + y


RINGS = [[ctx_of(x, z, y) for z in range(NZ)] for x in range(NX) for y in range(NY)]
PLANES = [[ctx_of(x, z, y) for x in range(NX) for y in range(NY)] for z in range(NZ)]

ROW_W = 512
ROW_LIVE = 640
ROWS_B = 656
ROW_EXTRA = 256
ROWS_C = 272
ROW_PLANE = 272
ROWS_D = 400
ROW_GW = 512
ROWS_E = 640
ROWS_A = 288
ROWS_F = 416


def iota(shape, dim):
    return lax.broadcasted_iota(jnp.int32, shape, dim)


def fiota(shape, dim):
    return iota(shape, dim).astype(F32)


def dot(a, b):
    return jnp.dot(a, b, preferred_element_type=F32)


def dot_nt(a, b):
    return lax.dot_general(a, b, (((1,), (1,)), ((), ())), preferred_element_type=F32)


def dot_tn(a, b):
    return lax.dot_general(a, b, (((0,), (0,)), ((), ())), preferred_element_type=F32)


def ones_where(mask):
    return jnp.where(mask, 1.0, 0.0).astype(BF)


def swap_matrix():
    dest = iota((TOK, TOK), 0)
    source = ((dest >> 1) & 7) * 16 + (dest >> 4) * 2 + (dest & 1)
    return ones_where(iota((TOK, TOK), 1) == source)


def three_parts(spread, lane):
    high = spread.astype(BF).astype(F32)
    rest = spread - high
    middle = rest.astype(BF).astype(F32)
    low = rest - middle
    return jnp.where(lane < 16, high, jnp.where(lane < 32, middle, jnp.where(lane < 48, low, 0.0)))


def split_slot(slot):
    owner = jnp.floor(slot * (1.0 / 16.0))
    inside = slot - 16.0 * owner
    bucket = jnp.floor(inside * 0.5)
    return owner, bucket, inside - 2.0 * bucket


def pack_ring(qk_in, v_in, w_in, b_in, msg_ref, qk_ref, v_ref, w_ref, b_ref, sems):
    fetches = [
        pltpu.make_async_copy(source, dest, sems.at[n])
        for n, (source, dest) in enumerate(((qk_in, qk_ref), (v_in, v_ref), (w_in, w_ref), (b_in, b_ref)))
    ]
    for fetch in fetches:
        fetch.start()
    fetches[3].wait()
    rows = jnp.concatenate([b_ref[...].astype(F32), jnp.zeros((14, TOK), F32)], axis=0).astype(BF)
    for z in range(NZ):
        msg_ref[z, 272:288, :] = rows
    for fetch, ref, span in zip(fetches, (qk_ref, v_ref, w_ref), ((0, 128), (128, 256), (256, 272))):
        fetch.wait()
        for z in range(NZ):
            msg_ref[z, slice(*span), :] = ref[:, z * DIM : (z + 1) * DIM]


def route(a_ref, slot_out, msg_out, slot_ref, y_ref, msg_ref, sems):
    sub = iota((TOK, TOK), 0)
    lane = iota((TOK, TOK), 1)
    swap = swap_matrix()
    slot_sub = fiota((SLOTS, TOK), 0)
    live = jnp.zeros((SLOTS, TOK), F32)
    scols = jnp.zeros((TOK, TOK), F32)
    for z in range(NZ):
        rows = jnp.concatenate([a_ref[z, 0:128, :], a_ref[z, 128:256, :]], axis=1)
        places, marks = [], []
        for r in range(ROUNDS):
            brow = a_ref[z, 272:288, :].astype(F32)[r : r + 1, :]
            bcol = jnp.sum(jnp.where(sub == lane, brow, 0.0), axis=1, keepdims=True)
            same = jnp.where(bcol == brow, 1.0, 0.0)
            prow = jnp.sum(jnp.where(sub < lane, same, 0.0), axis=0, keepdims=True)
            pcol = jnp.sum(jnp.where(lane < sub, same, 0.0), axis=1, keepdims=True)
            srow = 2.0 * brow + prow
            scol = 2.0 * bcol + pcol
            slot_ref[r * NZ + z : r * NZ + z + 1, :] = srow
            scols = jnp.where(lane == r * NZ + z, scol, scols)
            y_ref[r, z] = dot(ones_where(slot_sub == srow), rows).astype(BF)
            owner, _, _ = split_slot(srow)
            places.append(ones_where(slot_sub == owner * 16.0 + (2.0 * z) + prow))
            _, bucket, _ = split_slot(scol)
            marks.append(ones_where(lane.astype(F32) == bucket + (1.0 * r * BUCKETS)))
        live = live + dot(jnp.concatenate(places, axis=1), jnp.concatenate(marks, axis=0))
    slot_ref[16:144, :] = scols
    keeps = [pltpu.make_async_copy(slot_ref, slot_out, sems.at[NG])]
    keeps[0].start()
    live = live.astype(BF)
    for o in range(NG):
        for r in range(ROUNDS):
            block = y_ref[r, :, o * 16 : (o + 1) * 16, :].reshape(TOK, 2 * DIM)
            moved = dot(swap, block).astype(BF)
            msg_ref[o, r * 128 : (r + 1) * 128, :] = moved[:, :DIM]
            msg_ref[o, 256 + r * 128 : 256 + (r + 1) * 128, :] = moved[:, DIM:]
        msg_ref[o, ROW_LIVE:ROWS_B, :] = live[o * 16 : (o + 1) * 16, :]
        for z in range(NZ):
            msg_ref[o, ROW_W + z * 16 : ROW_W + (z + 1) * 16, :] = a_ref[z, 256:272, :]
        keeps.append(pltpu.make_async_copy(msg_ref.at[o], msg_out.at[o], sems.at[o]))
        keeps[-1].start()
    for keep in keeps:
        keep.wait()


def raw_scores(q):
    scores = dot_nt(q, q) * SCALE
    itself = iota((SLOTS, SLOTS), 0) == iota((SLOTS, SLOTS), 1)
    return jnp.where(itself, scores - SELF_PENALTY, scores)


def bucket_rows(ref, start):
    return ref[:, start : start + 16, :].reshape(SLOTS, DIM)


def attend(b_ref, state_out, msg_ref, w_ref, state_ref, sem):
    lane = iota((SLOTS, TOK), 1)
    live = bucket_rows(b_ref, ROW_LIVE)

    def order(j):
        return (j >> 6) * 64 + ((j >> 1) & 7) * 8 + ((j >> 4) & 3) * 2 + (j & 1)

    earlier = ones_where(order(iota((SLOTS, SLOTS), 1)) < order(iota((SLOTS, SLOTS), 0)))
    rank = dot(earlier, live)
    span = jnp.where(rank >= 128.0, 1.0, 0.0)
    kcol = jnp.where(live.astype(F32) > 0.5, span, 2.0).astype(BF)
    pick = ones_where(iota((16, TOK), 0) == iota((16, TOK), 1))
    krows = dot_nt(pick, kcol)
    logs = jnp.zeros((SLOTS, TOK), F32)
    for r in range(ROUNDS):
        for k in range(BUCKETS):
            n = r * BUCKETS + k
            q = bucket_rows(b_ref, r * 128 + k * 16)
            v = bucket_rows(b_ref, 256 + r * 128 + k * 16)
            scores = jnp.where(krows[n : n + 1, :] <= span[:, n : n + 1], raw_scores(q), MASKED)
            largest = jnp.max(scores, axis=1, keepdims=True)
            lifted = jnp.exp(scores - largest)
            summed = jnp.sum(lifted, axis=1, keepdims=True)
            probability = (lifted * (1.0 / summed)).astype(BF)
            out = dot(probability, v).astype(BF)
            msg_ref[:, r * 128 + k * 16 : r * 128 + (k + 1) * 16, :] = out.reshape(NG, 16, DIM)
            logs = jnp.where((lane & 15) == n, largest + jnp.log(summed), logs)
    shifted = dot_nt(span.astype(BF), ones_where(iota((TOK, TOK), 0) == iota((TOK, TOK), 1) + 16))
    state_ref[0:256, :] = jnp.where(lane < 16, logs, shifted)
    state_ref[256:272, :] = krows[:, 0:128]
    state_ref[272:288, :] = krows[:, 128:256]
    keep = pltpu.make_async_copy(state_ref, state_out, sem)
    keep.start()
    msg_ref[:, ROW_EXTRA:ROWS_C, :] = three_parts(logs, lane).astype(BF).reshape(NG, 16, DIM)
    for x in range(NX):
        for y in range(NY):
            for z in range(NZ):
                at = ctx_of(x, z, y) * 16
                w_ref[at : at + 16, :] = b_ref[x * NY + y, ROW_W + z * 16 : ROW_W + (z + 1) * 16, :]
    keep.wait()


def recall(b_ref, state_ref, prob_ref, turned_ref, mark_ref):
    krows = jnp.concatenate([state_ref[256:272, :], state_ref[272:288, :]], axis=1)
    for n in range(ROUNDS * BUCKETS):
        q = bucket_rows(b_ref, n * 16)
        seen = krows[n : n + 1, :] <= state_ref[0:256, 16 + n : 17 + n]
        scores = jnp.where(seen, raw_scores(q), MASKED)
        probability = jnp.exp(scores - state_ref[0:256, n : n + 1])
        prob_ref[n] = probability
        turned_ref[n] = probability.T.astype(BF)
    mark_ref[...] = krows[0:8, 0:128]


def combine(
    z_ref, slot_in, weight_in, c_ref, grad_ref, turned_out, msg_out, att_ref,
    y_ref, s_ref, slot_ref, weight_ref, turned_ref, msg_ref, sems,
):
    fetch = pltpu.make_async_copy(slot_in, slot_ref, sems.at[NZ])
    fetch.start()
    fetch_weight = pltpu.make_async_copy(weight_in, weight_ref, sems.at[NZ + 1])
    fetch_weight.start()
    keeps = []
    lane = iota((TOK, TOK), 1)
    swap = swap_matrix()
    slot_sub = fiota((SLOTS, TOK), 0)
    slot_lane = fiota((TOK, SLOTS), 1)
    for o in range(NG):
        rows = jnp.concatenate([c_ref[o, 0:128, :], c_ref[o, 128:256, :]], axis=1)
        y_ref[:, o * 16 : (o + 1) * 16, :] = dot(swap, rows).astype(BF).reshape(NZ, 16, 2 * DIM)
    log_rows = bucket_rows(c_ref, ROW_EXTRA)
    extra = jnp.zeros((SLOTS, TOK), F32)
    folded = (lane & 15).astype(F32)
    fetch.wait()
    for z in range(NZ):
        outs, logs, marks = [], [], []
        for r in range(ROUNDS):
            n = r * NZ + z
            scol = slot_ref[16:144, n : n + 1]
            outs.append(dot(ones_where(slot_lane == scol), y_ref[z, :, r * DIM : (r + 1) * DIM]))
            owner, bucket, place = split_slot(scol)
            parts = dot(ones_where(slot_lane == owner * 16.0 + (2.0 * z) + place), log_rows)
            marks.append(folded == bucket + (1.0 * r * BUCKETS))
            logs.append(jnp.sum(jnp.where(marks[r], parts, 0.0), axis=1, keepdims=True))
        largest = jnp.maximum(logs[0], logs[1])
        lifted = [jnp.exp(log - largest) for log in logs]
        total = lifted[0] + lifted[1]
        weights = [one / total for one in lifted]
        att = (weights[0] * outs[0] + weights[1] * outs[1]).astype(BF)
        att_ref[z * TOK : (z + 1) * TOK, :] = att
        turned = pl.ds(pl.multiple_of(lax.rem(z_ref[0] - z + NZ, NZ) * TOK, TOK), TOK)
        turned_ref[z * TOK : (z + 1) * TOK, :] = att
        keeps.append(
            pltpu.make_async_copy(turned_ref.at[z * TOK : (z + 1) * TOK, :], turned_out.at[turned, :], sems.at[z])
        )
        keeps[-1].start()
        grad = grad_ref[turned, :]
        inner = jnp.sum(grad * att.astype(F32), axis=1, keepdims=True)
        for r in range(ROUNDS):
            n = r * NZ + z
            srow = slot_ref[n : n + 1, :]
            query_grad = (weights[r] * grad).astype(BF)
            s_ref[z, :, r * DIM : (r + 1) * DIM] = dot(ones_where(slot_sub == srow), query_grad).astype(BF)
            owner, _, place = split_slot(srow)
            spread = jnp.where(marks[r], weights[r] * inner, 0.0)
            extra = extra + dot(
                ones_where(slot_sub == owner * 16.0 + (2.0 * z) + place),
                three_parts(spread, lane).astype(BF),
            )
    fetch_weight.wait()
    extra = extra.astype(BF)
    for o in range(NG):
        moved = dot(swap, s_ref[:, o * 16 : (o + 1) * 16, :].reshape(TOK, 2 * DIM)).astype(BF)
        msg_ref[o, 0:128, :] = moved[:, :DIM]
        msg_ref[o, 128:256, :] = moved[:, DIM:]
        msg_ref[o, ROW_EXTRA:ROWS_C, :] = extra[o * 16 : (o + 1) * 16, :]
        for h in range(NZ):
            msg_ref[o, ROW_PLANE + h * 16 : ROW_PLANE + (h + 1) * 16, :] = weight_ref[:, h * DIM : (h + 1) * DIM]
        keeps.append(pltpu.make_async_copy(msg_ref.at[o], msg_out.at[o], sems.at[NZ + 2 + o]))
        keeps[-1].start()
    for keep in keeps:
        keep.wait()


def attend_back(d_in, b_ref, prob_ref, turned_ref, gw_ref, msg_ref, mark_ref, d_ref, sems):
    fetches = [
        pltpu.make_async_copy(d_in.at[:, rows, :], d_ref.at[:, rows, :], sems.at[n])
        for n, rows in enumerate((slice(ROW_EXTRA, ROWS_C), slice(0, 128), slice(128, 256)))
    ]
    for fetch in fetches:
        fetch.start()
    for x in range(NX):
        for y in range(NY):
            for z in range(NZ):
                at = ctx_of(x, z, y) * 16
                msg_ref[x * NY + y, ROW_GW + z * 16 : ROW_GW + (z + 1) * 16, :] = gw_ref[at : at + 16, :]
    lane = iota((SLOTS, TOK), 1)
    fetches[0].wait()
    shifts = bucket_rows(d_ref, ROW_EXTRA).astype(F32)
    for r in range(ROUNDS):
        fetches[1 + r].wait()
        for k in range(BUCKETS):
            n = r * BUCKETS + k
            q = bucket_rows(b_ref, n * 16)
            v = bucket_rows(b_ref, 256 + n * 16)
            g = bucket_rows(d_ref, n * 16)
            shift = jnp.sum(jnp.where((lane & 15) == n, shifts, 0.0), axis=1, keepdims=True)
            score_grad = (prob_ref[n] * (dot_nt(g, v) - shift)).astype(BF)
            qk_grad = (dot(score_grad, q) + dot_tn(score_grad, q)) * SCALE
            value_grad = dot(turned_ref[n], g)
            msg_ref[:, n * 16 : (n + 1) * 16, :] = qk_grad.astype(BF).reshape(NG, 16, DIM)
            rows = slice(256 + n * 16, 256 + (n + 1) * 16)
            msg_ref[:, rows, :] = value_grad.astype(BF).reshape(NG, 16, DIM)
    mark_ref[...] = shifts[0:8, :]


def join(*refs):
    out_ref, sems = refs[NZ:]
    copies = [
        pltpu.make_async_copy(ref, out_ref.at[n * TOK : (n + 1) * TOK, :], sems.at[n])
        for n, ref in enumerate(refs[:NZ])
    ]
    for copy in copies:
        copy.start()
    for copy in copies:
        copy.wait()


def project(place_ref, d_ref, *refs):
    own_out, other_out, plane_ref, att_ref, sem, sems = refs[NZ:]
    fetch = pltpu.make_async_copy(d_ref.at[:, ROW_PLANE:ROWS_D, :], plane_ref, sem)
    fetch.start()
    blocks = [
        pltpu.make_async_copy(ref, att_ref.at[:, n * DIM : (n + 1) * DIM], sems.at[n])
        for n, ref in enumerate(refs[:NZ])
    ]
    for block in blocks:
        block.start()
    fetch.wait()
    weights = []
    for core in (place_ref[0], 1 - place_ref[0]):
        parts = []
        for turn in range(NZ):
            head = lax.rem(place_ref[1] - turn + NZ, NZ)
            rows = pl.ds(pl.multiple_of(head * 16, 16), 16)
            parts.append(plane_ref[pl.ds(core * (NG // 2), NG // 2), rows, :].reshape(NG * 8, DIM))
        weights.append(jnp.concatenate(parts, axis=1))
    weights = jnp.concatenate(weights, axis=0)
    for block in blocks:
        block.wait()
    for z in range(NZ):
        tokens = slice(z * TOK, (z + 1) * TOK)
        both = dot_nt(att_ref[tokens, :], weights)
        own_out[tokens, :] = both[:, :DIM]
        other_out[tokens, :] = both[:, DIM:]


def gather_home(slot_in, own_in, other_in, e_ref, msg_ref, y_ref, slot_ref, own_ref, other_ref, sems):
    fetches = [
        pltpu.make_async_copy(source, dest, sems.at[n])
        for n, (source, dest) in enumerate(((slot_in, slot_ref), (own_in, own_ref), (other_in, other_ref)))
    ]
    for fetch in fetches:
        fetch.start()
    swap = swap_matrix()
    slot_lane = fiota((TOK, SLOTS), 1)
    for r in range(ROUNDS):
        for o in range(NG):
            rows = jnp.concatenate(
                [
                    e_ref[o, r * 128 : (r + 1) * 128, :],
                    e_ref[o, 256 + r * 128 : 256 + (r + 1) * 128, :],
                ],
                axis=1,
            )
            at = r * SLOTS + o * 16
            y_ref[:, at : at + 16, :] = dot(swap, rows).astype(BF).reshape(NZ, 16, 2 * DIM)
    total = jnp.zeros((TOK, DIM), F32)
    for o in range(NG):
        total = total + e_ref[o, ROW_GW:ROWS_E, :].astype(F32)
    total = total * (1.0 / math.sqrt(NX * NY * NZ * TOK))
    high = total.astype(BF)
    low = (total - high.astype(F32)).astype(BF)
    fetches[0].wait()
    for z in range(NZ):
        picks = [ones_where(slot_lane == slot_ref[16:144, n : n + 1]) for n in (z, NZ + z)]
        rows = dot(jnp.concatenate(picks, axis=1), y_ref[z]).astype(BF)
        msg_ref[z, 0:128, :] = rows[:, :DIM]
        msg_ref[z, 128:256, :] = rows[:, DIM:]
        msg_ref[z, 384:400, :] = high[z * 16 : (z + 1) * 16, :]
        msg_ref[z, 400:416, :] = low[z * 16 : (z + 1) * 16, :]
    fetches[1].wait()
    fetches[2].wait()
    for z in range(NZ):
        tokens = slice(z * TOK, (z + 1) * TOK)
        msg_ref[z, 256:384, :] = (own_ref[tokens, :] + other_ref[tokens, :]).astype(BF)


def unpack_ring(f_ref, qk_ref, v_ref, mixed_ref, gw_ref):
    for z in range(NZ):
        cols = slice(z * DIM, (z + 1) * DIM)
        qk_ref[:, cols] = f_ref[z, 0:128, :]
        v_ref[:, cols] = f_ref[z, 128:256, :]
        gw_ref[:, cols] = f_ref[z, 384:400, :].astype(F32) + f_ref[z, 400:416, :].astype(F32)
    for z in range(0, NZ, 2):
        first, second = f_ref[z, 256:384, :], f_ref[z + 1, 256:384, :]
        for half in range(2):
            cols = slice(half * 512 + z * 64, half * 512 + z * 64 + 128)
            part = slice(half * 64, half * 64 + 64)
            mixed_ref[:, cols] = jnp.concatenate([first[:, part], second[:, part]], axis=1)


def on_device(body, outs, scratch=(), scalars=0, hbm_in=0, hbm_out=0, vmem=24, cost=None, pin=True):
    shapes = [
        pltpu.HBM(shape, kind) if n < hbm_out else jax.ShapeDtypeStruct(shape, kind)
        for n, (shape, kind) in enumerate(outs)
    ]
    scratches = [pltpu.VMEM(*one) if isinstance(one, tuple) else one for one in scratch]

    def call(*operands):
        operands = [
            pltpu.with_memory_space_constraint(one, pltpu.HBM) if pin and scalars <= n < scalars + hbm_in else one
            for n, one in enumerate(operands)
        ]
        places = [pltpu.SMEM] * scalars + [pltpu.HBM] * hbm_in
        places += [pltpu.VMEM] * (len(operands) - len(places))
        return pl.pallas_call(
            body,
            out_shape=shapes,
            in_specs=[pl.BlockSpec(memory_space=place) for place in places],
            out_specs=[
                pl.BlockSpec(memory_space=pltpu.HBM if n < hbm_out else pltpu.VMEM) for n in range(len(shapes))
            ],
            scratch_shapes=scratches,
            cost_estimate=None if cost is None else pl.CostEstimate(
                flops=cost[0], bytes_accessed=cost[1], transcendentals=cost[2]
            ),
            compiler_params=pltpu.CompilerParams(vmem_limit_bytes=vmem * 1024 * 1024),
        )(*operands)

    return call


def exchange(message, groups):
    return lax.all_to_all(
        message, "ctx", split_axis=0, concat_axis=0, tiled=True, axis_index_groups=groups
    )


def swap_cores(array):
    return lax.ppermute(array, "head", [(0, 1), (1, 0)])


def pass_on(block, step):
    turn = [
        (ctx_of(x, z, y), ctx_of(x, (z + step) % NZ, y)) for x in range(NX) for z in range(NZ) for y in range(NY)
    ]
    return lax.ppermute(block, "ctx", turn)


def ring_round(forward, backward):
    return pass_on(forward, 1), pass_on(backward, -1)


def after(arrays, event):
    return lax.optimization_barrier((*arrays, event))[: len(arrays)]


def per_device(shared_qk, values, out_grad, out_weight, buckets):
    core = lax.axis_index("head")
    z_place = lax.rem(lax.axis_index("ctx") // NY, NZ)
    width = shared_qk.shape[1]

    (msg,) = on_device(
        pack_ring,
        [((NZ, ROWS_A, DIM), BF)],
        [
            ((TOK, width), BF),
            ((TOK, width), BF),
            ((16, width), BF),
            (buckets.shape, jnp.int32),
            pltpu.SemaphoreType.DMA((4,)),
        ],
        hbm_in=4,
    )(shared_qk, values, out_weight, buckets)
    got_a = exchange(msg, RINGS)
    slots, msg = on_device(
        route,
        [((16 + TOK, TOK), F32), ((NG, ROWS_B, DIM), BF)],
        [
            ((16 + TOK, TOK), F32),
            ((ROUNDS, NZ, SLOTS, 2 * DIM), BF),
            ((NG, ROWS_B, DIM), BF),
            pltpu.SemaphoreType.DMA((NG + 1,)),
        ],
        hbm_out=2,
    )(got_a)
    late_grad, msg = lax.optimization_barrier((out_grad, msg))
    got_b = exchange(msg, PLANES)
    before1, after1 = ring_round(late_grad, late_grad)
    before2, after2 = ring_round(before1, after1)
    before3, after3 = ring_round(before2, after2)
    before4 = pass_on(before3, 1)
    blocks = [late_grad, before1, before2, before3, before4, after3, after2, after1]
    (ring_grad,) = on_device(
        join, [((NZ * TOK, width), BF)], [pltpu.SemaphoreType.DMA((NZ,))], hbm_in=NZ, hbm_out=1, pin=False
    )(*blocks)
    state, msg, head_weight = on_device(
        attend,
        [((SLOTS + 32, TOK), F32), ((NG, ROWS_C, DIM), BF), ((2 * width, DIM), BF)],
        [((SLOTS + 32, TOK), F32), pltpu.SemaphoreType.DMA],
        hbm_out=1,
    )(got_b)
    got_c = exchange(msg, PLANES)
    other_grad = swap_cores(ring_grad)
    own_part = lax.dynamic_slice_in_dim(head_weight, core * width, width, 0)
    other_part = lax.dynamic_slice_in_dim(head_weight, (1 - core) * width, width, 0)
    attended_grad = dot(ring_grad, own_part) + dot(other_grad, other_part)
    turned, msg, attended = on_device(
        combine,
        [((NZ * TOK, DIM), BF), ((NG, ROWS_D, DIM), BF), ((NZ * TOK, DIM), BF)],
        [
            ((NZ, SLOTS, 2 * DIM), BF),
            ((NZ, SLOTS, 2 * DIM), BF),
            ((16 + TOK, TOK), F32),
            ((16, width), BF),
            ((NZ * TOK, DIM), BF),
            ((NG, ROWS_D, DIM), BF),
            pltpu.SemaphoreType.DMA((NZ + 2 + NG,)),
        ],
        scalars=1,
        hbm_in=2,
        hbm_out=2,
    )(z_place.reshape(1), slots, out_weight, got_c, attended_grad)
    got_d = exchange(msg, PLANES)
    att_before1, att_after1 = ring_round(attended, attended)
    att_before2, att_after2 = ring_round(att_before1, att_after1)
    own_gw = dot_tn(ring_grad, turned).astype(BF)
    other_gw = dot_tn(other_grad, turned).astype(BF)
    both_gw = jnp.concatenate(
        [jnp.where(core == 0, own_gw, other_gw), jnp.where(core == 0, other_gw, own_gw)], axis=0
    )
    got_d, att_before2, att_after2 = lax.optimization_barrier((got_d, att_before2, att_after2))
    state, att_before2, att_after2 = lax.optimization_barrier((state, att_before2, att_after2))
    buckets_here = ROUNDS * BUCKETS
    probability, probability_turned, _ = on_device(
        recall,
        [((buckets_here, SLOTS, SLOTS), F32), ((buckets_here, SLOTS, SLOTS), BF), ((8, TOK), F32)],
        cost=(2 * buckets_here * SLOTS * SLOTS * DIM, 8 << 20, buckets_here * SLOTS * SLOTS),
    )(got_b, state)
    msg, mark = on_device(
        attend_back,
        [((NG, ROWS_E, DIM), BF), ((8, TOK), F32)],
        [((NG, ROWS_C, DIM), BF), pltpu.SemaphoreType.DMA((3,))],
        hbm_in=1,
    )(got_d, got_b, probability, probability_turned, both_gw)
    got_e = exchange(msg, PLANES)
    late_before2, late_after2 = after((att_before2, att_after2), mark)
    att_before3, att_after3 = ring_round(late_before2, late_after2)
    att_before4 = pass_on(att_before3, 1)
    all_attended = [attended, att_before1, att_before2, att_before3, att_before4]
    all_attended += [att_after3, att_after2, att_after1]
    own_rows, other_rows = on_device(
        project,
        [((NZ * TOK, DIM), F32), ((NZ * TOK, DIM), F32)],
        [
            ((NG, ROWS_D - ROW_PLANE, DIM), BF),
            ((NZ * TOK, width), BF),
            pltpu.SemaphoreType.DMA,
            pltpu.SemaphoreType.DMA((NZ,)),
        ],
        scalars=1,
        hbm_in=1 + NZ,
    )(jnp.stack([core, z_place]), got_d, *all_attended)
    other_rows = swap_cores(other_rows)
    (msg,) = on_device(
        gather_home,
        [((NZ, ROWS_F, DIM), BF)],
        [
            ((NZ, ROUNDS * SLOTS, 2 * DIM), BF),
            ((16 + TOK, TOK), F32),
            ((NZ * TOK, DIM), F32),
            ((NZ * TOK, DIM), F32),
            pltpu.SemaphoreType.DMA((3,)),
        ],
        hbm_in=3,
    )(slots, own_rows, other_rows, got_e)
    got_f = exchange(msg, RINGS)
    grad_qk, grad_values, mixed, grad_weight = on_device(
        unpack_ring,
        [((TOK, width), BF), ((TOK, width), BF), ((TOK, width), BF), ((16, width), F32)],
    )(got_f)
    return (mixed, grad_qk, grad_values, grad_weight)


def solution(mesh):
    assert mesh.shape["ctx"] == NX * NY * NZ and mesh.shape["head"] == 2
    in_specs = (
        P("ctx", "head"),
        P("ctx", "head"),
        P("ctx", "head"),
        P("ctx", "head"),
        P(None, "ctx"),
    )
    out_specs = (P("ctx", "head"), P("ctx", "head"), P("ctx", "head"), P("ctx", "head"))
    return jax.shard_map(
        per_device, mesh=mesh, in_specs=in_specs, out_specs=out_specs, check_vma=False
    )
```

```python
import math

import jax
import jax.numpy as jnp
from jax import lax
from jax.experimental import pallas as pl
from jax.experimental.pallas import tpu as pltpu
from jax.sharding import PartitionSpec as P

NX, NZ, NY = 4, 8, 4
NG = NX * NY
TOK = 128
DIM = 128
ROUNDS = 2
BUCKETS = 8
SLOTS = 256
SCALE = DIM ** (-0.5)
SELF_PENALTY = 10000.0
MASKED = -1e30
BF = jnp.bfloat16
F32 = jnp.float32


def ctx_of(x, z, y):
    return (x * NZ + z) * NY + y


RINGS = [[ctx_of(x, z, y) for z in range(NZ)] for x in range(NX) for y in range(NY)]
PLANES = [[ctx_of(x, z, y) for x in range(NX) for y in range(NY)] for z in range(NZ)]

ROW_W = 512
ROW_LIVE = 640
ROWS_B = 656
ROW_EXTRA = 256
ROWS_C = 272
ROW_PLANE = 272
ROWS_D = 400
ROWS_E = 512
ROWS_A = 288
ROWS_F = 384


def iota(shape, dim):
    return lax.broadcasted_iota(jnp.int32, shape, dim)


def fiota(shape, dim):
    return iota(shape, dim).astype(F32)


def dot(a, b):
    return jnp.dot(a, b, preferred_element_type=F32)


def dot_nt(a, b):
    return lax.dot_general(a, b, (((1,), (1,)), ((), ())), preferred_element_type=F32)


def dot_tn(a, b):
    return lax.dot_general(a, b, (((0,), (0,)), ((), ())), preferred_element_type=F32)


def ones_where(mask):
    return jnp.where(mask, 1.0, 0.0).astype(BF)


def swap_matrix():
    dest = iota((TOK, TOK), 0)
    source = ((dest >> 1) & 7) * 16 + (dest >> 4) * 2 + (dest & 1)
    return ones_where(iota((TOK, TOK), 1) == source)


def three_parts(spread, lane):
    high = spread.astype(BF).astype(F32)
    rest = spread - high
    middle = rest.astype(BF).astype(F32)
    low = rest - middle
    return jnp.where(lane < 16, high, jnp.where(lane < 32, middle, jnp.where(lane < 48, low, 0.0)))


def split_slot(slot):
    owner = jnp.floor(slot * (1.0 / 16.0))
    inside = slot - 16.0 * owner
    bucket = jnp.floor(inside * 0.5)
    return owner, bucket, inside - 2.0 * bucket


def pack_ring(qk_in, v_in, w_in, b_in, msg_ref, qk_ref, v_ref, w_ref, b_ref, sems):
    fetches = [
        pltpu.make_async_copy(source, dest, sems.at[n])
        for n, (source, dest) in enumerate(((qk_in, qk_ref), (v_in, v_ref), (w_in, w_ref), (b_in, b_ref)))
    ]
    for fetch in fetches:
        fetch.start()
    fetches[3].wait()
    rows = jnp.concatenate([b_ref[...].astype(F32), jnp.zeros((14, TOK), F32)], axis=0).astype(BF)
    for z in range(NZ):
        msg_ref[z, 272:288, :] = rows
    for fetch, ref, span in zip(fetches, (qk_ref, v_ref, w_ref), ((0, 128), (128, 256), (256, 272))):
        fetch.wait()
        for z in range(NZ):
            msg_ref[z, slice(*span), :] = ref[:, z * DIM : (z + 1) * DIM]


def route(a_ref, slot_out, msg_out, slot_ref, y_ref, msg_ref, sems):
    sub = iota((TOK, TOK), 0)
    lane = iota((TOK, TOK), 1)
    swap = swap_matrix()
    slot_sub = fiota((SLOTS, TOK), 0)
    live = jnp.zeros((SLOTS, TOK), F32)
    scols = jnp.zeros((TOK, TOK), F32)
    for z in range(NZ):
        rows = jnp.concatenate([a_ref[z, 0:128, :], a_ref[z, 128:256, :]], axis=1)
        places, marks = [], []
        for r in range(ROUNDS):
            brow = a_ref[z, 272:288, :].astype(F32)[r : r + 1, :]
            bcol = jnp.sum(jnp.where(sub == lane, brow, 0.0), axis=1, keepdims=True)
            same = jnp.where(bcol == brow, 1.0, 0.0)
            prow = jnp.sum(jnp.where(sub < lane, same, 0.0), axis=0, keepdims=True)
            pcol = jnp.sum(jnp.where(lane < sub, same, 0.0), axis=1, keepdims=True)
            srow = 2.0 * brow + prow
            scol = 2.0 * bcol + pcol
            slot_ref[r * NZ + z : r * NZ + z + 1, :] = srow
            scols = jnp.where(lane == r * NZ + z, scol, scols)
            y_ref[r, z] = dot(ones_where(slot_sub == srow), rows).astype(BF)
            owner, _, _ = split_slot(srow)
            places.append(ones_where(slot_sub == owner * 16.0 + (2.0 * z) + prow))
            _, bucket, _ = split_slot(scol)
            marks.append(ones_where(lane.astype(F32) == bucket + (1.0 * r * BUCKETS)))
        live = live + dot(jnp.concatenate(places, axis=1), jnp.concatenate(marks, axis=0))
    slot_ref[16:144, :] = scols
    keeps = [pltpu.make_async_copy(slot_ref, slot_out, sems.at[NG])]
    keeps[0].start()
    live = live.astype(BF)
    for o in range(NG):
        for r in range(ROUNDS):
            block = y_ref[r, :, o * 16 : (o + 1) * 16, :].reshape(TOK, 2 * DIM)
            moved = dot(swap, block).astype(BF)
            msg_ref[o, r * 128 : (r + 1) * 128, :] = moved[:, :DIM]
            msg_ref[o, 256 + r * 128 : 256 + (r + 1) * 128, :] = moved[:, DIM:]
        msg_ref[o, ROW_LIVE:ROWS_B, :] = live[o * 16 : (o + 1) * 16, :]
        for z in range(NZ):
            msg_ref[o, ROW_W + z * 16 : ROW_W + (z + 1) * 16, :] = a_ref[z, 256:272, :]
        keeps.append(pltpu.make_async_copy(msg_ref.at[o], msg_out.at[o], sems.at[o]))
        keeps[-1].start()
    for keep in keeps:
        keep.wait()


def raw_scores(q):
    scores = dot_nt(q, q) * SCALE
    itself = iota((SLOTS, SLOTS), 0) == iota((SLOTS, SLOTS), 1)
    return jnp.where(itself, scores - SELF_PENALTY, scores)


def bucket_rows(ref, start):
    return ref[:, start : start + 16, :].reshape(SLOTS, DIM)


def attend(b_ref, state_out, msg_ref, w_ref, state_ref, sem):
    lane = iota((SLOTS, TOK), 1)
    live = bucket_rows(b_ref, ROW_LIVE)

    def order(j):
        return (j >> 6) * 64 + ((j >> 1) & 7) * 8 + ((j >> 4) & 3) * 2 + (j & 1)

    earlier = ones_where(order(iota((SLOTS, SLOTS), 1)) < order(iota((SLOTS, SLOTS), 0)))
    rank = dot(earlier, live)
    span = jnp.where(rank >= 128.0, 1.0, 0.0)
    kcol = jnp.where(live.astype(F32) > 0.5, span, 2.0).astype(BF)
    pick = ones_where(iota((16, TOK), 0) == iota((16, TOK), 1))
    krows = dot_nt(pick, kcol)
    logs = jnp.zeros((SLOTS, TOK), F32)
    for r in range(ROUNDS):
        for k in range(BUCKETS):
            n = r * BUCKETS + k
            q = bucket_rows(b_ref, r * 128 + k * 16)
            v = bucket_rows(b_ref, 256 + r * 128 + k * 16)
            scores = jnp.where(krows[n : n + 1, :] <= span[:, n : n + 1], raw_scores(q), MASKED)
            largest = jnp.max(scores, axis=1, keepdims=True)
            lifted = jnp.exp(scores - largest)
            summed = jnp.sum(lifted, axis=1, keepdims=True)
            probability = (lifted * (1.0 / summed)).astype(BF)
            out = dot(probability, v).astype(BF)
            msg_ref[:, r * 128 + k * 16 : r * 128 + (k + 1) * 16, :] = out.reshape(NG, 16, DIM)
            logs = jnp.where((lane & 15) == n, largest + jnp.log(summed), logs)
    shifted = dot_nt(span.astype(BF), ones_where(iota((TOK, TOK), 0) == iota((TOK, TOK), 1) + 16))
    state_ref[0:256, :] = jnp.where(lane < 16, logs, shifted)
    state_ref[256:272, :] = krows[:, 0:128]
    state_ref[272:288, :] = krows[:, 128:256]
    keep = pltpu.make_async_copy(state_ref, state_out, sem)
    keep.start()
    msg_ref[:, ROW_EXTRA:ROWS_C, :] = three_parts(logs, lane).astype(BF).reshape(NG, 16, DIM)
    for x in range(NX):
        for y in range(NY):
            for z in range(NZ):
                at = ctx_of(x, z, y) * 16
                w_ref[at : at + 16, :] = b_ref[x * NY + y, ROW_W + z * 16 : ROW_W + (z + 1) * 16, :]
    keep.wait()


def recall(b_ref, state_ref, prob_ref, turned_ref, mark_ref):
    krows = jnp.concatenate([state_ref[256:272, :], state_ref[272:288, :]], axis=1)
    for n in range(ROUNDS * BUCKETS):
        q = bucket_rows(b_ref, n * 16)
        seen = krows[n : n + 1, :] <= state_ref[0:256, 16 + n : 17 + n]
        scores = jnp.where(seen, raw_scores(q), MASKED)
        probability = jnp.exp(scores - state_ref[0:256, n : n + 1])
        prob_ref[n] = probability
        turned_ref[n] = probability.T.astype(BF)
    mark_ref[...] = krows[0:8, 0:128]


def combine(
    z_ref, slot_in, weight_in, c_ref, grad_ref, msg_out, att_ref,
    y_ref, s_ref, slot_ref, weight_ref, msg_ref, sems,
):
    fetch = pltpu.make_async_copy(slot_in, slot_ref, sems.at[NZ])
    fetch.start()
    fetch_weight = pltpu.make_async_copy(weight_in, weight_ref, sems.at[NZ + 1])
    fetch_weight.start()
    keeps = []
    lane = iota((TOK, TOK), 1)
    swap = swap_matrix()
    slot_sub = fiota((SLOTS, TOK), 0)
    slot_lane = fiota((TOK, SLOTS), 1)
    for o in range(NG):
        rows = jnp.concatenate([c_ref[o, 0:128, :], c_ref[o, 128:256, :]], axis=1)
        y_ref[:, o * 16 : (o + 1) * 16, :] = dot(swap, rows).astype(BF).reshape(NZ, 16, 2 * DIM)
    log_rows = bucket_rows(c_ref, ROW_EXTRA)
    extra = jnp.zeros((SLOTS, TOK), F32)
    folded = (lane & 15).astype(F32)
    fetch.wait()
    for z in range(NZ):
        outs, logs, marks = [], [], []
        for r in range(ROUNDS):
            n = r * NZ + z
            scol = slot_ref[16:144, n : n + 1]
            outs.append(dot(ones_where(slot_lane == scol), y_ref[z, :, r * DIM : (r + 1) * DIM]))
            owner, bucket, place = split_slot(scol)
            parts = dot(ones_where(slot_lane == owner * 16.0 + (2.0 * z) + place), log_rows)
            marks.append(folded == bucket + (1.0 * r * BUCKETS))
            logs.append(jnp.sum(jnp.where(marks[r], parts, 0.0), axis=1, keepdims=True))
        largest = jnp.maximum(logs[0], logs[1])
        lifted = [jnp.exp(log - largest) for log in logs]
        total = lifted[0] + lifted[1]
        weights = [one / total for one in lifted]
        att = (weights[0] * outs[0] + weights[1] * outs[1]).astype(BF)
        att_ref[z * TOK : (z + 1) * TOK, :] = att
        turned = pl.ds(pl.multiple_of(lax.rem(z_ref[0] - z + NZ, NZ) * TOK, TOK), TOK)
        grad = grad_ref[turned, :]
        inner = jnp.sum(grad * att.astype(F32), axis=1, keepdims=True)
        for r in range(ROUNDS):
            n = r * NZ + z
            srow = slot_ref[n : n + 1, :]
            query_grad = (weights[r] * grad).astype(BF)
            s_ref[z, :, r * DIM : (r + 1) * DIM] = dot(ones_where(slot_sub == srow), query_grad).astype(BF)
            owner, _, place = split_slot(srow)
            spread = jnp.where(marks[r], weights[r] * inner, 0.0)
            extra = extra + dot(
                ones_where(slot_sub == owner * 16.0 + (2.0 * z) + place),
                three_parts(spread, lane).astype(BF),
            )
    fetch_weight.wait()
    extra = extra.astype(BF)
    for o in range(NG):
        moved = dot(swap, s_ref[:, o * 16 : (o + 1) * 16, :].reshape(TOK, 2 * DIM)).astype(BF)
        msg_ref[o, 0:128, :] = moved[:, :DIM]
        msg_ref[o, 128:256, :] = moved[:, DIM:]
        msg_ref[o, ROW_EXTRA:ROWS_C, :] = extra[o * 16 : (o + 1) * 16, :]
        for h in range(NZ):
            msg_ref[o, ROW_PLANE + h * 16 : ROW_PLANE + (h + 1) * 16, :] = weight_ref[:, h * DIM : (h + 1) * DIM]
        keeps.append(pltpu.make_async_copy(msg_ref.at[o], msg_out.at[o], sems.at[NZ + 2 + o]))
        keeps[-1].start()
    for keep in keeps:
        keep.wait()


def attend_back(d_in, b_ref, prob_ref, turned_ref, msg_ref, mark_ref, d_ref, sems):
    fetches = [
        pltpu.make_async_copy(d_in.at[:, rows, :], d_ref.at[:, rows, :], sems.at[n])
        for n, rows in enumerate((slice(ROW_EXTRA, ROWS_C), slice(0, 128), slice(128, 256)))
    ]
    for fetch in fetches:
        fetch.start()
    lane = iota((SLOTS, TOK), 1)
    fetches[0].wait()
    shifts = bucket_rows(d_ref, ROW_EXTRA).astype(F32)
    for r in range(ROUNDS):
        fetches[1 + r].wait()
        for k in range(BUCKETS):
            n = r * BUCKETS + k
            q = bucket_rows(b_ref, n * 16)
            v = bucket_rows(b_ref, 256 + n * 16)
            g = bucket_rows(d_ref, n * 16)
            shift = jnp.sum(jnp.where((lane & 15) == n, shifts, 0.0), axis=1, keepdims=True)
            score_grad = (prob_ref[n] * (dot_nt(g, v) - shift)).astype(BF)
            qk_grad = (dot(score_grad, q) + dot_tn(score_grad, q)) * SCALE
            value_grad = dot(turned_ref[n], g)
            msg_ref[:, n * 16 : (n + 1) * 16, :] = qk_grad.astype(BF).reshape(NG, 16, DIM)
            rows = slice(256 + n * 16, 256 + (n + 1) * 16)
            msg_ref[:, rows, :] = value_grad.astype(BF).reshape(NG, 16, DIM)
    mark_ref[...] = shifts[0:8, :]


def join(*refs):
    out_ref, sems = refs[NZ:]
    copies = [
        pltpu.make_async_copy(ref, out_ref.at[n * TOK : (n + 1) * TOK, :], sems.at[n])
        for n, ref in enumerate(refs[:NZ])
    ]
    for copy in copies:
        copy.start()
    for copy in copies:
        copy.wait()


def project(place_ref, d_ref, turned_in, *refs):
    own_out, other_out = refs[NZ : NZ + 2]
    outs = refs[NZ + 2 : NZ + 2 + NX]
    plane_ref, att_ref, turned_ref, sems = refs[NZ + 2 + NX :]
    blocks = []
    for n, ref in enumerate(refs[:NZ]):
        head = lax.rem(place_ref[1] - n + NZ, NZ)
        blocks.append(pltpu.make_async_copy(ref, att_ref.at[head], sems.at[n]))
    fetch = pltpu.make_async_copy(d_ref.at[:, ROW_PLANE:ROWS_D, :], plane_ref, sems.at[NZ])
    fetch_turned = pltpu.make_async_copy(turned_in, turned_ref, sems.at[NZ + 1])
    for copy in (fetch, *blocks, fetch_turned):
        copy.start()
    fetch.wait()
    weights = []
    for core in (place_ref[0], 1 - place_ref[0]):
        parts = []
        for head in range(NZ):
            rows = plane_ref[pl.ds(core * (NG // 2), NG // 2), head * 16 : (head + 1) * 16, :]
            parts.append(rows.reshape(NG * 8, DIM))
        weights.append(jnp.concatenate(parts, axis=1))
    weights = jnp.concatenate(weights, axis=0)
    for block in blocks:
        block.wait()
    for z in range(NZ):
        tokens = slice(z * TOK, (z + 1) * TOK)
        rows = jnp.concatenate([att_ref[head, tokens, :] for head in range(NZ)], axis=1)
        both = dot_nt(rows, weights)
        own_out[tokens, :] = both[:, :DIM]
        other_out[tokens, :] = both[:, DIM:]
    fetch_turned.wait()
    for head in range(NZ):
        part = dot(turned_ref[...], att_ref[head]).astype(BF)
        for step in range(NX):
            outs[step][:, head * DIM : (head + 1) * DIM] = part[step * 64 : (step + 1) * 64, :]


def turn_grad(place_ref, own_in, other_in, out_ref, og_ref, sems):
    core, z_here, x_here = place_ref[0], place_ref[1], place_ref[2]
    fetches = []
    for step in range(NX):
        x = lax.rem(x_here + step, NX)
        at = pl.multiple_of(lax.rem(x, 2) * (NZ * 64) + (z_here // 2) * TOK, TOK)
        mine = x // 2 == core
        own, other = [
            pltpu.make_async_copy(source.at[:, pl.ds(at, TOK)], og_ref.at[step], sems.at[step])
            for source in (own_in, other_in)
        ]
        pl.when(mine)(own.start)
        pl.when(jnp.logical_not(mine))(other.start)
        fetches.append(own)
    odd = lax.rem(z_here, 2) == 1
    for fetch in fetches:
        fetch.wait()
    for step in range(NX):
        for z in range(NZ):
            turn = pl.multiple_of(lax.rem(z_here - z + NZ, NZ) * TOK, TOK)
            rows = og_ref[step, pl.ds(turn, TOK), :].astype(F32).T
            rows = jnp.where(odd, rows[64:128, :], rows[0:64, :]).astype(BF)
            out_ref[step * 64 : (step + 1) * 64, z * TOK : (z + 1) * TOK] = rows


def fold(place_ref, *refs):
    total_ref = refs[2 * NY]
    total = refs[0][...].astype(F32)
    for ref in refs[1:NX]:
        total = total + ref[...].astype(F32)
    total_ref[...] = total * (1.0 / math.sqrt(NX * NY * NZ * TOK))
    for step, out in enumerate(refs[NX : NX + NY]):
        row = lax.rem(place_ref[3] + step, NY) * 16
        out[...] = total_ref[pl.ds(pl.multiple_of(row, 16), 16), :]


def gather_home(slot_in, mixed_in, e_ref, msg_ref, y_ref, slot_ref, mixed_ref, sems):
    fetches = [
        pltpu.make_async_copy(source, dest, sems.at[n])
        for n, (source, dest) in enumerate(((slot_in, slot_ref), (mixed_in, mixed_ref)))
    ]
    for fetch in fetches:
        fetch.start()
    swap = swap_matrix()
    slot_lane = fiota((TOK, SLOTS), 1)
    for r in range(ROUNDS):
        for o in range(NG):
            rows = jnp.concatenate(
                [
                    e_ref[o, r * 128 : (r + 1) * 128, :],
                    e_ref[o, 256 + r * 128 : 256 + (r + 1) * 128, :],
                ],
                axis=1,
            )
            at = r * SLOTS + o * 16
            y_ref[:, at : at + 16, :] = dot(swap, rows).astype(BF).reshape(NZ, 16, 2 * DIM)
    fetches[0].wait()
    for z in range(NZ):
        picks = [ones_where(slot_lane == slot_ref[16:144, n : n + 1]) for n in (z, NZ + z)]
        rows = dot(jnp.concatenate(picks, axis=1), y_ref[z]).astype(BF)
        msg_ref[z, 0:128, :] = rows[:, :DIM]
        msg_ref[z, 128:256, :] = rows[:, DIM:]
    fetches[1].wait()
    for z in range(NZ):
        msg_ref[z, 256:384, :] = mixed_ref[z * TOK : (z + 1) * TOK, :]


def unpack_ring(f_ref, qk_ref, v_ref, mixed_ref):
    for z in range(NZ):
        cols = slice(z * DIM, (z + 1) * DIM)
        qk_ref[:, cols] = f_ref[z, 0:128, :]
        v_ref[:, cols] = f_ref[z, 128:256, :]
    for z in range(0, NZ, 2):
        first, second = f_ref[z, 256:384, :], f_ref[z + 1, 256:384, :]
        for half in range(2):
            cols = slice(half * 512 + z * 64, half * 512 + z * 64 + 128)
            part = slice(half * 64, half * 64 + 64)
            mixed_ref[:, cols] = jnp.concatenate([first[:, part], second[:, part]], axis=1)


def on_device(body, outs, scratch=(), scalars=0, hbm_in=0, hbm_out=0, vmem=24, cost=None, pin=True):
    shapes = [
        pltpu.HBM(shape, kind) if n < hbm_out else jax.ShapeDtypeStruct(shape, kind)
        for n, (shape, kind) in enumerate(outs)
    ]
    scratches = [pltpu.VMEM(*one) if isinstance(one, tuple) else one for one in scratch]

    def call(*operands):
        operands = [
            pltpu.with_memory_space_constraint(one, pltpu.HBM) if pin and scalars <= n < scalars + hbm_in else one
            for n, one in enumerate(operands)
        ]
        places = [pltpu.SMEM] * scalars + [pltpu.HBM] * hbm_in
        places += [pltpu.VMEM] * (len(operands) - len(places))
        return pl.pallas_call(
            body,
            out_shape=shapes,
            in_specs=[pl.BlockSpec(memory_space=place) for place in places],
            out_specs=[
                pl.BlockSpec(memory_space=pltpu.HBM if n < hbm_out else pltpu.VMEM) for n in range(len(shapes))
            ],
            scratch_shapes=scratches,
            cost_estimate=None if cost is None else pl.CostEstimate(
                flops=cost[0], bytes_accessed=cost[1], transcendentals=cost[2]
            ),
            compiler_params=pltpu.CompilerParams(vmem_limit_bytes=vmem * 1024 * 1024),
        )(*operands)

    return call


def exchange(message, groups):
    return lax.all_to_all(
        message, "ctx", split_axis=0, concat_axis=0, tiled=True, axis_index_groups=groups
    )


def swap_cores(array):
    return lax.ppermute(array, "head", [(0, 1), (1, 0)])


def pass_on(block, z_step, x_step=0, y_step=0):
    turn = [
        (ctx_of(x, z, y), ctx_of((x + x_step) % NX, (z + z_step) % NZ, (y + y_step) % NY))
        for x in range(NX)
        for z in range(NZ)
        for y in range(NY)
    ]
    return lax.ppermute(block, "ctx", turn)


def ring_round(forward, backward):
    return pass_on(forward, 1), pass_on(backward, -1)


def after(arrays, event):
    return lax.optimization_barrier((*arrays, event))[: len(arrays)]


def per_device(shared_qk, values, out_grad, out_weight, buckets):
    core = lax.axis_index("head")
    place = lax.axis_index("ctx")
    x_place, z_place, y_place = place // (NZ * NY), lax.rem(place // NY, NZ), lax.rem(place, NY)
    width = shared_qk.shape[1]

    (msg,) = on_device(
        pack_ring,
        [((NZ, ROWS_A, DIM), BF)],
        [
            ((TOK, width), BF),
            ((TOK, width), BF),
            ((16, width), BF),
            (buckets.shape, jnp.int32),
            pltpu.SemaphoreType.DMA((4,)),
        ],
        hbm_in=4,
    )(shared_qk, values, out_weight, buckets)
    got_a = exchange(msg, RINGS)
    slots, msg = on_device(
        route,
        [((16 + TOK, TOK), F32), ((NG, ROWS_B, DIM), BF)],
        [
            ((16 + TOK, TOK), F32),
            ((ROUNDS, NZ, SLOTS, 2 * DIM), BF),
            ((NG, ROWS_B, DIM), BF),
            pltpu.SemaphoreType.DMA((NG + 1,)),
        ],
        hbm_out=2,
    )(got_a)
    late_grad, msg = lax.optimization_barrier((out_grad, msg))
    got_b = exchange(msg, PLANES)
    before1, after1 = ring_round(late_grad, late_grad)
    before2, after2 = ring_round(before1, after1)
    before3, after3 = ring_round(before2, after2)
    before4 = pass_on(before3, 1)
    blocks = [late_grad, before1, before2, before3, before4, after3, after2, after1]
    (ring_grad,) = on_device(
        join, [((NZ * TOK, width), BF)], [pltpu.SemaphoreType.DMA((NZ,))], hbm_in=NZ, hbm_out=1, pin=False
    )(*blocks)
    state, msg, head_weight = on_device(
        attend,
        [((SLOTS + 32, TOK), F32), ((NG, ROWS_C, DIM), BF), ((2 * width, DIM), BF)],
        [((SLOTS + 32, TOK), F32), pltpu.SemaphoreType.DMA],
        hbm_out=1,
    )(got_b)
    got_c = exchange(msg, PLANES)
    other_grad = swap_cores(ring_grad)
    own_part = lax.dynamic_slice_in_dim(head_weight, core * width, width, 0)
    other_part = lax.dynamic_slice_in_dim(head_weight, (1 - core) * width, width, 0)
    attended_grad = dot(ring_grad, own_part) + dot(other_grad, other_part)
    places = jnp.stack([core, z_place, x_place, y_place])
    (grad_turned,) = on_device(
        turn_grad,
        [((NX * 64, NZ * TOK), BF)],
        [((NX, NZ * TOK, TOK), BF), pltpu.SemaphoreType.DMA((NX,))],
        scalars=1,
        hbm_in=2,
    )(places, ring_grad, other_grad)
    got_c, grad_turned = lax.optimization_barrier((got_c, grad_turned))
    msg, attended = on_device(
        combine,
        [((NG, ROWS_D, DIM), BF), ((NZ * TOK, DIM), BF)],
        [
            ((NZ, SLOTS, 2 * DIM), BF),
            ((NZ, SLOTS, 2 * DIM), BF),
            ((16 + TOK, TOK), F32),
            ((16, width), BF),
            ((NG, ROWS_D, DIM), BF),
            pltpu.SemaphoreType.DMA((NZ + 2 + NG,)),
        ],
        scalars=1,
        hbm_in=2,
        hbm_out=1,
    )(z_place.reshape(1), slots, out_weight, got_c, attended_grad)
    got_d = exchange(msg, PLANES)
    att_before1, att_after1 = ring_round(attended, attended)
    att_before2, att_after2 = ring_round(att_before1, att_after1)
    got_d, att_before2, att_after2 = lax.optimization_barrier((got_d, att_before2, att_after2))
    state, att_before2, att_after2 = lax.optimization_barrier((state, att_before2, att_after2))
    buckets_here = ROUNDS * BUCKETS
    probability, probability_turned, _ = on_device(
        recall,
        [((buckets_here, SLOTS, SLOTS), F32), ((buckets_here, SLOTS, SLOTS), BF), ((8, TOK), F32)],
        cost=(2 * buckets_here * SLOTS * SLOTS * DIM, 8 << 20, buckets_here * SLOTS * SLOTS),
    )(got_b, state)
    msg, mark = on_device(
        attend_back,
        [((NG, ROWS_E, DIM), BF), ((8, TOK), F32)],
        [((NG, ROWS_C, DIM), BF), pltpu.SemaphoreType.DMA((3,))],
        hbm_in=1,
    )(got_d, got_b, probability, probability_turned)
    got_e = exchange(msg, PLANES)
    late_before2, late_after2 = after((att_before2, att_after2), mark)
    att_before3, att_after3 = ring_round(late_before2, late_after2)
    att_before4 = pass_on(att_before3, 1)
    all_attended = [attended, att_before1, att_before2, att_before3, att_before4]
    all_attended += [att_after3, att_after2, att_after1]
    own_rows, other_rows, *parts = on_device(
        project,
        [((NZ * TOK, DIM), F32)] * 2 + [((64, width), BF)] * NX,
        [
            ((NG, ROWS_D - ROW_PLANE, DIM), BF),
            ((NZ, NZ * TOK, DIM), BF),
            ((NX * 64, NZ * TOK), BF),
            pltpu.SemaphoreType.DMA((NZ + 2,)),
        ],
        scalars=1,
        hbm_in=2 + NZ,
    )(places, got_d, grad_turned, *all_attended)
    mixed_rows = (own_rows + swap_cores(other_rows)).astype(BF)
    (msg,) = on_device(
        gather_home,
        [((NZ, ROWS_F, DIM), BF)],
        [
            ((NZ, ROUNDS * SLOTS, 2 * DIM), BF),
            ((16 + TOK, TOK), F32),
            ((NZ * TOK, DIM), BF),
            pltpu.SemaphoreType.DMA((2,)),
        ],
        hbm_in=2,
    )(slots, mixed_rows, got_e)
    got_f = exchange(msg, RINGS)
    parts = [parts[0]] + [pass_on(parts[step], 0, x_step=step) for step in range(1, NX)]
    sums = on_device(fold, [((16, width), F32)] * NY, [((64, width), F32)], scalars=1)(places, *parts)
    sums = [sums[0]] + [pass_on(sums[step], 0, y_step=step) for step in range(1, NY)]
    grad_weight = sums[0] + sums[1] + sums[2] + sums[3]
    grad_qk, grad_values, mixed = on_device(unpack_ring, [((TOK, width), BF)] * 3)(got_f)
    return (mixed, grad_qk, grad_values, grad_weight)


def solution(mesh):
    assert mesh.shape["ctx"] == NX * NY * NZ and mesh.shape["head"] == 2
    in_specs = (
        P("ctx", "head"),
        P("ctx", "head"),
        P("ctx", "head"),
        P("ctx", "head"),
        P(None, "ctx"),
    )
    out_specs = (P("ctx", "head"), P("ctx", "head"), P("ctx", "head"), P("ctx", "head"))
    return jax.shard_map(
        per_device, mesh=mesh, in_specs=in_specs, out_specs=out_specs, check_vma=False
    )
```

```python
import math

import jax
import jax.numpy as jnp
from jax import lax
from jax.experimental import pallas as pl
from jax.experimental.pallas import tpu as pltpu
from jax.sharding import PartitionSpec as P

NX, NZ, NY = 4, 8, 4
NG = NX * NY
TOK = 128
DIM = 128
ROUNDS = 2
BUCKETS = 8
SLOTS = 256
SCALE = DIM ** (-0.5)
SELF_PENALTY = 10000.0
MASKED = -1e30
BF = jnp.bfloat16
F32 = jnp.float32


def ctx_of(x, z, y):
    return (x * NZ + z) * NY + y


RINGS = [[ctx_of(x, z, y) for z in range(NZ)] for x in range(NX) for y in range(NY)]
PLANES = [[ctx_of(x, z, y) for x in range(NX) for y in range(NY)] for z in range(NZ)]

ROW_W = 512
ROW_LIVE = 640
ROWS_B = 656
ROW_EXTRA = 256
ROWS_C = 272
ROW_PLANE = 272
ROWS_D = 400
ROW_GW = 512
ROWS_E = 640
ROWS_A = 288
ROWS_F = 416


def iota(shape, dim):
    return lax.broadcasted_iota(jnp.int32, shape, dim)


def fiota(shape, dim):
    return iota(shape, dim).astype(F32)


def dot(a, b):
    return jnp.dot(a, b, preferred_element_type=F32)


def dot_nt(a, b):
    return lax.dot_general(a, b, (((1,), (1,)), ((), ())), preferred_element_type=F32)


def dot_tn(a, b):
    return lax.dot_general(a, b, (((0,), (0,)), ((), ())), preferred_element_type=F32)


def ones_where(mask):
    return jnp.where(mask, 1.0, 0.0).astype(BF)


def swap_matrix():
    dest = iota((TOK, TOK), 0)
    source = ((dest >> 1) & 7) * 16 + (dest >> 4) * 2 + (dest & 1)
    return ones_where(iota((TOK, TOK), 1) == source)


def three_parts(spread, lane):
    high = spread.astype(BF).astype(F32)
    rest = spread - high
    middle = rest.astype(BF).astype(F32)
    low = rest - middle
    return jnp.where(lane < 16, high, jnp.where(lane < 32, middle, jnp.where(lane < 48, low, 0.0)))


def split_slot(slot):
    owner = jnp.floor(slot * (1.0 / 16.0))
    inside = slot - 16.0 * owner
    bucket = jnp.floor(inside * 0.5)
    return owner, bucket, inside - 2.0 * bucket


def pack_ring(qk_in, v_in, w_in, b_in, msg_ref, qk_ref, v_ref, w_ref, b_ref, sems):
    fetches = [
        pltpu.make_async_copy(source, dest, sems.at[n])
        for n, (source, dest) in enumerate(((qk_in, qk_ref), (v_in, v_ref), (w_in, w_ref), (b_in, b_ref)))
    ]
    for fetch in fetches:
        fetch.start()
    fetches[3].wait()
    rows = jnp.concatenate([b_ref[...].astype(F32), jnp.zeros((14, TOK), F32)], axis=0).astype(BF)
    for z in range(NZ):
        msg_ref[z, 272:288, :] = rows
    for fetch, ref, span in zip(fetches, (qk_ref, v_ref, w_ref), ((0, 128), (128, 256), (256, 272))):
        fetch.wait()
        for z in range(NZ):
            msg_ref[z, slice(*span), :] = ref[:, z * DIM : (z + 1) * DIM]


def route(a_ref, slot_out, msg_out, slot_ref, y_ref, msg_ref, sems):
    sub = iota((TOK, TOK), 0)
    lane = iota((TOK, TOK), 1)
    swap = swap_matrix()
    slot_sub = fiota((SLOTS, TOK), 0)
    live = jnp.zeros((SLOTS, TOK), F32)
    scols = jnp.zeros((TOK, TOK), F32)
    for z in range(NZ):
        rows = jnp.concatenate([a_ref[z, 0:128, :], a_ref[z, 128:256, :]], axis=1)
        places, marks = [], []
        for r in range(ROUNDS):
            brow = a_ref[z, 272:288, :].astype(F32)[r : r + 1, :]
            bcol = jnp.sum(jnp.where(sub == lane, brow, 0.0), axis=1, keepdims=True)
            same = jnp.where(bcol == brow, 1.0, 0.0)
            prow = jnp.sum(jnp.where(sub < lane, same, 0.0), axis=0, keepdims=True)
            pcol = jnp.sum(jnp.where(lane < sub, same, 0.0), axis=1, keepdims=True)
            srow = 2.0 * brow + prow
            scol = 2.0 * bcol + pcol
            slot_ref[r * NZ + z : r * NZ + z + 1, :] = srow
            scols = jnp.where(lane == r * NZ + z, scol, scols)
            y_ref[r, z] = dot(ones_where(slot_sub == srow), rows).astype(BF)
            owner, _, _ = split_slot(srow)
            places.append(ones_where(slot_sub == owner * 16.0 + (2.0 * z) + prow))
            _, bucket, _ = split_slot(scol)
            marks.append(ones_where(lane.astype(F32) == bucket + (1.0 * r * BUCKETS)))
        live = live + dot(jnp.concatenate(places, axis=1), jnp.concatenate(marks, axis=0))
    slot_ref[16:144, :] = scols
    keeps = [pltpu.make_async_copy(slot_ref, slot_out, sems.at[NG])]
    keeps[0].start()
    live = live.astype(BF)
    for o in range(NG):
        for r in range(ROUNDS):
            block = y_ref[r, :, o * 16 : (o + 1) * 16, :].reshape(TOK, 2 * DIM)
            moved = dot(swap, block).astype(BF)
            msg_ref[o, r * 128 : (r + 1) * 128, :] = moved[:, :DIM]
            msg_ref[o, 256 + r * 128 : 256 + (r + 1) * 128, :] = moved[:, DIM:]
        msg_ref[o, ROW_LIVE:ROWS_B, :] = live[o * 16 : (o + 1) * 16, :]
        for z in range(NZ):
            msg_ref[o, ROW_W + z * 16 : ROW_W + (z + 1) * 16, :] = a_ref[z, 256:272, :]
        keeps.append(pltpu.make_async_copy(msg_ref.at[o], msg_out.at[o], sems.at[o]))
        keeps[-1].start()
    for keep in keeps:
        keep.wait()


def raw_scores(q):
    scores = dot_nt(q, q) * SCALE
    itself = iota((SLOTS, SLOTS), 0) == iota((SLOTS, SLOTS), 1)
    return jnp.where(itself, scores - SELF_PENALTY, scores)


def bucket_rows(ref, start):
    return ref[:, start : start + 16, :].reshape(SLOTS, DIM)


def attend(b_ref, state_out, msg_ref, w_ref, state_ref, sem):
    lane = iota((SLOTS, TOK), 1)
    live = bucket_rows(b_ref, ROW_LIVE)

    def order(j):
        return (j >> 6) * 64 + ((j >> 1) & 7) * 8 + ((j >> 4) & 3) * 2 + (j & 1)

    earlier = ones_where(order(iota((SLOTS, SLOTS), 1)) < order(iota((SLOTS, SLOTS), 0)))
    rank = dot(earlier, live)
    span = jnp.where(rank >= 128.0, 1.0, 0.0)
    kcol = jnp.where(live.astype(F32) > 0.5, span, 2.0).astype(BF)
    pick = ones_where(iota((16, TOK), 0) == iota((16, TOK), 1))
    krows = dot_nt(pick, kcol)
    logs = jnp.zeros((SLOTS, TOK), F32)
    for r in range(ROUNDS):
        for k in range(BUCKETS):
            n = r * BUCKETS + k
            q = bucket_rows(b_ref, r * 128 + k * 16)
            v = bucket_rows(b_ref, 256 + r * 128 + k * 16)
            scores = jnp.where(krows[n : n + 1, :] <= span[:, n : n + 1], raw_scores(q), MASKED)
            largest = jnp.max(scores, axis=1, keepdims=True)
            lifted = jnp.exp(scores - largest)
            summed = jnp.sum(lifted, axis=1, keepdims=True)
            probability = (lifted * (1.0 / summed)).astype(BF)
            out = dot(probability, v).astype(BF)
            msg_ref[:, r * 128 + k * 16 : r * 128 + (k + 1) * 16, :] = out.reshape(NG, 16, DIM)
            logs = jnp.where((lane & 15) == n, largest + jnp.log(summed), logs)
    shifted = dot_nt(span.astype(BF), ones_where(iota((TOK, TOK), 0) == iota((TOK, TOK), 1) + 16))
    state_ref[0:256, :] = jnp.where(lane < 16, logs, shifted)
    state_ref[256:272, :] = krows[:, 0:128]
    state_ref[272:288, :] = krows[:, 128:256]
    keep = pltpu.make_async_copy(state_ref, state_out, sem)
    keep.start()
    msg_ref[:, ROW_EXTRA:ROWS_C, :] = three_parts(logs, lane).astype(BF).reshape(NG, 16, DIM)
    for x in range(NX):
        for y in range(NY):
            for z in range(NZ):
                at = ctx_of(x, z, y) * 16
                w_ref[at : at + 16, :] = b_ref[x * NY + y, ROW_W + z * 16 : ROW_W + (z + 1) * 16, :]
    keep.wait()


def recall(b_ref, state_ref, prob_ref, turned_ref, mark_ref):
    krows = jnp.concatenate([state_ref[256:272, :], state_ref[272:288, :]], axis=1)
    for n in range(ROUNDS * BUCKETS):
        q = bucket_rows(b_ref, n * 16)
        seen = krows[n : n + 1, :] <= state_ref[0:256, 16 + n : 17 + n]
        scores = jnp.where(seen, raw_scores(q), MASKED)
        probability = jnp.exp(scores - state_ref[0:256, n : n + 1])
        prob_ref[n] = probability
        turned_ref[n] = probability.T.astype(BF)
    mark_ref[...] = krows[0:8, 0:128]


def combine(
    z_ref, slot_in, weight_in, c_ref, grad_ref, turned_out, msg_out, att_ref,
    y_ref, s_ref, slot_ref, weight_ref, turned_ref, msg_ref, sems,
):
    fetch = pltpu.make_async_copy(slot_in, slot_ref, sems.at[NZ])
    fetch.start()
    fetch_weight = pltpu.make_async_copy(weight_in, weight_ref, sems.at[NZ + 1])
    fetch_weight.start()
    keeps = []
    lane = iota((TOK, TOK), 1)
    swap = swap_matrix()
    slot_sub = fiota((SLOTS, TOK), 0)
    slot_lane = fiota((TOK, SLOTS), 1)
    for o in range(NG):
        rows = jnp.concatenate([c_ref[o, 0:128, :], c_ref[o, 128:256, :]], axis=1)
        y_ref[:, o * 16 : (o + 1) * 16, :] = dot(swap, rows).astype(BF).reshape(NZ, 16, 2 * DIM)
    log_rows = bucket_rows(c_ref, ROW_EXTRA)
    extra = jnp.zeros((SLOTS, TOK), F32)
    folded = (lane & 15).astype(F32)
    fetch.wait()
    for z in range(NZ):
        outs, logs, marks = [], [], []
        for r in range(ROUNDS):
            n = r * NZ + z
            scol = slot_ref[16:144, n : n + 1]
            outs.append(dot(ones_where(slot_lane == scol), y_ref[z, :, r * DIM : (r + 1) * DIM]))
            owner, bucket, place = split_slot(scol)
            parts = dot(ones_where(slot_lane == owner * 16.0 + (2.0 * z) + place), log_rows)
            marks.append(folded == bucket + (1.0 * r * BUCKETS))
            logs.append(jnp.sum(jnp.where(marks[r], parts, 0.0), axis=1, keepdims=True))
        largest = jnp.maximum(logs[0], logs[1])
        lifted = [jnp.exp(log - largest) for log in logs]
        total = lifted[0] + lifted[1]
        weights = [one / total for one in lifted]
        att = (weights[0] * outs[0] + weights[1] * outs[1]).astype(BF)
        att_ref[z * TOK : (z + 1) * TOK, :] = att
        turned = pl.ds(pl.multiple_of(lax.rem(z_ref[0] - z + NZ, NZ) * TOK, TOK), TOK)
        turned_ref[z * TOK : (z + 1) * TOK, :] = att
        keeps.append(
            pltpu.make_async_copy(turned_ref.at[z * TOK : (z + 1) * TOK, :], turned_out.at[turned, :], sems.at[z])
        )
        keeps[-1].start()
        grad = grad_ref[turned, :]
        inner = jnp.sum(grad * att.astype(F32), axis=1, keepdims=True)
        for r in range(ROUNDS):
            n = r * NZ + z
            srow = slot_ref[n : n + 1, :]
            query_grad = (weights[r] * grad).astype(BF)
            s_ref[z, :, r * DIM : (r + 1) * DIM] = dot(ones_where(slot_sub == srow), query_grad).astype(BF)
            owner, _, place = split_slot(srow)
            spread = jnp.where(marks[r], weights[r] * inner, 0.0)
            extra = extra + dot(
                ones_where(slot_sub == owner * 16.0 + (2.0 * z) + place),
                three_parts(spread, lane).astype(BF),
            )
    fetch_weight.wait()
    extra = extra.astype(BF)
    for o in range(NG):
        moved = dot(swap, s_ref[:, o * 16 : (o + 1) * 16, :].reshape(TOK, 2 * DIM)).astype(BF)
        msg_ref[o, 0:128, :] = moved[:, :DIM]
        msg_ref[o, 128:256, :] = moved[:, DIM:]
        msg_ref[o, ROW_EXTRA:ROWS_C, :] = extra[o * 16 : (o + 1) * 16, :]
        for h in range(NZ):
            msg_ref[o, ROW_PLANE + h * 16 : ROW_PLANE + (h + 1) * 16, :] = weight_ref[:, h * DIM : (h + 1) * DIM]
        keeps.append(pltpu.make_async_copy(msg_ref.at[o], msg_out.at[o], sems.at[NZ + 2 + o]))
        keeps[-1].start()
    for keep in keeps:
        keep.wait()


def attend_back(d_in, b_ref, prob_ref, turned_ref, gw_ref, msg_ref, mark_ref, d_ref, sems):
    fetches = [
        pltpu.make_async_copy(d_in.at[:, rows, :], d_ref.at[:, rows, :], sems.at[n])
        for n, rows in enumerate((slice(ROW_EXTRA, ROWS_C), slice(0, 128), slice(128, 256)))
    ]
    for fetch in fetches:
        fetch.start()
    for x in range(NX):
        for y in range(NY):
            for z in range(NZ):
                at = ctx_of(x, z, y) * 16
                msg_ref[x * NY + y, ROW_GW + z * 16 : ROW_GW + (z + 1) * 16, :] = gw_ref[at : at + 16, :]
    lane = iota((SLOTS, TOK), 1)
    fetches[0].wait()
    shifts = bucket_rows(d_ref, ROW_EXTRA).astype(F32)
    for r in range(ROUNDS):
        fetches[1 + r].wait()
        for k in range(BUCKETS):
            n = r * BUCKETS + k
            q = bucket_rows(b_ref, n * 16)
            v = bucket_rows(b_ref, 256 + n * 16)
            g = bucket_rows(d_ref, n * 16)
            shift = jnp.sum(jnp.where((lane & 15) == n, shifts, 0.0), axis=1, keepdims=True)
            score_grad = (prob_ref[n] * (dot_nt(g, v) - shift)).astype(BF)
            qk_grad = (dot(score_grad, q) + dot_tn(score_grad, q)) * SCALE
            value_grad = dot(turned_ref[n], g)
            msg_ref[:, n * 16 : (n + 1) * 16, :] = qk_grad.astype(BF).reshape(NG, 16, DIM)
            rows = slice(256 + n * 16, 256 + (n + 1) * 16)
            msg_ref[:, rows, :] = value_grad.astype(BF).reshape(NG, 16, DIM)
    mark_ref[...] = shifts[0:8, :]


def join(*refs):
    out_ref, sems = refs[NZ:]
    copies = [
        pltpu.make_async_copy(ref, out_ref.at[n * TOK : (n + 1) * TOK, :], sems.at[n])
        for n, ref in enumerate(refs[:NZ])
    ]
    for copy in copies:
        copy.start()
    for copy in copies:
        copy.wait()


def project(place_ref, d_ref, *refs):
    own_out, other_out, plane_ref, att_ref, sem, sems = refs[NZ:]
    fetch = pltpu.make_async_copy(d_ref.at[:, ROW_PLANE:ROWS_D, :], plane_ref, sem)
    fetch.start()
    blocks = [
        pltpu.make_async_copy(ref, att_ref.at[:, n * DIM : (n + 1) * DIM], sems.at[n])
        for n, ref in enumerate(refs[:NZ])
    ]
    for block in blocks:
        block.start()
    fetch.wait()
    weights = []
    for core in (place_ref[0], 1 - place_ref[0]):
        parts = []
        for turn in range(NZ):
            head = lax.rem(place_ref[1] - turn + NZ, NZ)
            rows = pl.ds(pl.multiple_of(head * 16, 16), 16)
            parts.append(plane_ref[pl.ds(core * (NG // 2), NG // 2), rows, :].reshape(NG * 8, DIM))
        weights.append(jnp.concatenate(parts, axis=1))
    weights = jnp.concatenate(weights, axis=0)
    for block in blocks:
        block.wait()
    for z in range(NZ):
        tokens = slice(z * TOK, (z + 1) * TOK)
        both = dot_nt(att_ref[tokens, :], weights)
        own_out[tokens, :] = both[:, :DIM]
        other_out[tokens, :] = both[:, DIM:]


def gather_home(slot_in, own_in, other_in, e_ref, msg_ref, y_ref, slot_ref, own_ref, other_ref, sems):
    fetches = [
        pltpu.make_async_copy(source, dest, sems.at[n])
        for n, (source, dest) in enumerate(((slot_in, slot_ref), (own_in, own_ref), (other_in, other_ref)))
    ]
    for fetch in fetches:
        fetch.start()
    swap = swap_matrix()
    slot_lane = fiota((TOK, SLOTS), 1)
    for r in range(ROUNDS):
        for o in range(NG):
            rows = jnp.concatenate(
                [
                    e_ref[o, r * 128 : (r + 1) * 128, :],
                    e_ref[o, 256 + r * 128 : 256 + (r + 1) * 128, :],
                ],
                axis=1,
            )
            at = r * SLOTS + o * 16
            y_ref[:, at : at + 16, :] = dot(swap, rows).astype(BF).reshape(NZ, 16, 2 * DIM)
    total = jnp.zeros((TOK, DIM), F32)
    for o in range(NG):
        total = total + e_ref[o, ROW_GW:ROWS_E, :].astype(F32)
    total = total * (1.0 / math.sqrt(NX * NY * NZ * TOK))
    high = total.astype(BF)
    low = (total - high.astype(F32)).astype(BF)
    fetches[0].wait()
    for z in range(NZ):
        picks = [ones_where(slot_lane == slot_ref[16:144, n : n + 1]) for n in (z, NZ + z)]
        rows = dot(jnp.concatenate(picks, axis=1), y_ref[z]).astype(BF)
        msg_ref[z, 0:128, :] = rows[:, :DIM]
        msg_ref[z, 128:256, :] = rows[:, DIM:]
        msg_ref[z, 384:400, :] = high[z * 16 : (z + 1) * 16, :]
        msg_ref[z, 400:416, :] = low[z * 16 : (z + 1) * 16, :]
    fetches[1].wait()
    fetches[2].wait()
    for z in range(NZ):
        tokens = slice(z * TOK, (z + 1) * TOK)
        msg_ref[z, 256:384, :] = (own_ref[tokens, :] + other_ref[tokens, :]).astype(BF)


def unpack_ring(f_ref, qk_ref, v_ref, mixed_ref, gw_ref):
    for z in range(NZ):
        cols = slice(z * DIM, (z + 1) * DIM)
        qk_ref[:, cols] = f_ref[z, 0:128, :]
        v_ref[:, cols] = f_ref[z, 128:256, :]
        gw_ref[:, cols] = f_ref[z, 384:400, :].astype(F32) + f_ref[z, 400:416, :].astype(F32)
    for z in range(0, NZ, 2):
        first, second = f_ref[z, 256:384, :], f_ref[z + 1, 256:384, :]
        for half in range(2):
            cols = slice(half * 512 + z * 64, half * 512 + z * 64 + 128)
            part = slice(half * 64, half * 64 + 64)
            mixed_ref[:, cols] = jnp.concatenate([first[:, part], second[:, part]], axis=1)


def on_device(body, outs, scratch=(), scalars=0, hbm_in=0, hbm_out=0, vmem=24, cost=None, pin=True):
    shapes = [
        pltpu.HBM(shape, kind) if n < hbm_out else jax.ShapeDtypeStruct(shape, kind)
        for n, (shape, kind) in enumerate(outs)
    ]
    scratches = [pltpu.VMEM(*one) if isinstance(one, tuple) else one for one in scratch]

    def call(*operands):
        operands = [
            pltpu.with_memory_space_constraint(one, pltpu.HBM) if pin and scalars <= n < scalars + hbm_in else one
            for n, one in enumerate(operands)
        ]
        places = [pltpu.SMEM] * scalars + [pltpu.HBM] * hbm_in
        places += [pltpu.VMEM] * (len(operands) - len(places))
        return pl.pallas_call(
            body,
            out_shape=shapes,
            in_specs=[pl.BlockSpec(memory_space=place) for place in places],
            out_specs=[
                pl.BlockSpec(memory_space=pltpu.HBM if n < hbm_out else pltpu.VMEM) for n in range(len(shapes))
            ],
            scratch_shapes=scratches,
            cost_estimate=None if cost is None else pl.CostEstimate(
                flops=cost[0], bytes_accessed=cost[1], transcendentals=cost[2]
            ),
            compiler_params=pltpu.CompilerParams(vmem_limit_bytes=vmem * 1024 * 1024),
        )(*operands)

    return call


def exchange(message, groups):
    return lax.all_to_all(
        message, "ctx", split_axis=0, concat_axis=0, tiled=True, axis_index_groups=groups
    )


def swap_cores(array):
    return lax.ppermute(array, "head", [(0, 1), (1, 0)])


def pass_on(block, step):
    turn = [
        (ctx_of(x, z, y), ctx_of(x, (z + step) % NZ, y)) for x in range(NX) for z in range(NZ) for y in range(NY)
    ]
    return lax.ppermute(block, "ctx", turn)


def ring_round(forward, backward):
    return pass_on(forward, 1), pass_on(backward, -1)


def after(arrays, event):
    return lax.optimization_barrier((*arrays, event))[: len(arrays)]


def per_device(shared_qk, values, out_grad, out_weight, buckets):
    core = lax.axis_index("head")
    z_place = lax.rem(lax.axis_index("ctx") // NY, NZ)
    width = shared_qk.shape[1]

    (msg,) = on_device(
        pack_ring,
        [((NZ, ROWS_A, DIM), BF)],
        [
            ((TOK, width), BF),
            ((TOK, width), BF),
            ((16, width), BF),
            (buckets.shape, jnp.int32),
            pltpu.SemaphoreType.DMA((4,)),
        ],
        hbm_in=4,
    )(shared_qk, values, out_weight, buckets)
    got_a = exchange(msg, RINGS)
    slots, msg = on_device(
        route,
        [((16 + TOK, TOK), F32), ((NG, ROWS_B, DIM), BF)],
        [
            ((16 + TOK, TOK), F32),
            ((ROUNDS, NZ, SLOTS, 2 * DIM), BF),
            ((NG, ROWS_B, DIM), BF),
            pltpu.SemaphoreType.DMA((NG + 1,)),
        ],
        hbm_out=2,
    )(got_a)
    late_grad, msg = lax.optimization_barrier((out_grad, msg))
    got_b = exchange(msg, PLANES)
    before1, after1 = ring_round(late_grad, late_grad)
    before2, after2 = ring_round(before1, after1)
    before3, after3 = ring_round(before2, after2)
    before4 = pass_on(before3, 1)
    blocks = [late_grad, before1, before2, before3, before4, after3, after2, after1]
    (ring_grad,) = on_device(
        join, [((NZ * TOK, width), BF)], [pltpu.SemaphoreType.DMA((NZ,))], hbm_in=NZ, hbm_out=1, pin=False
    )(*blocks)
    state, msg, head_weight = on_device(
        attend,
        [((SLOTS + 32, TOK), F32), ((NG, ROWS_C, DIM), BF), ((2 * width, DIM), BF)],
        [((SLOTS + 32, TOK), F32), pltpu.SemaphoreType.DMA],
        hbm_out=1,
    )(got_b)
    got_c = exchange(msg, PLANES)
    other_grad = swap_cores(ring_grad)
    own_part = lax.dynamic_slice_in_dim(head_weight, core * width, width, 0)
    other_part = lax.dynamic_slice_in_dim(head_weight, (1 - core) * width, width, 0)
    attended_grad = dot(ring_grad, own_part) + dot(other_grad, other_part)
    turned, msg, attended = on_device(
        combine,
        [((NZ * TOK, DIM), BF), ((NG, ROWS_D, DIM), BF), ((NZ * TOK, DIM), BF)],
        [
            ((NZ, SLOTS, 2 * DIM), BF),
            ((NZ, SLOTS, 2 * DIM), BF),
            ((16 + TOK, TOK), F32),
            ((16, width), BF),
            ((NZ * TOK, DIM), BF),
            ((NG, ROWS_D, DIM), BF),
            pltpu.SemaphoreType.DMA((NZ + 2 + NG,)),
        ],
        scalars=1,
        hbm_in=2,
        hbm_out=2,
    )(z_place.reshape(1), slots, out_weight, got_c, attended_grad)
    got_d = exchange(msg, PLANES)
    att_before1, att_after1 = ring_round(attended, attended)
    own_gw = dot_tn(ring_grad, turned).astype(BF)
    other_gw = dot_tn(other_grad, turned).astype(BF)
    both_gw = jnp.concatenate(
        [jnp.where(core == 0, own_gw, other_gw), jnp.where(core == 0, other_gw, own_gw)], axis=0
    )
    got_d, att_before1, att_after1 = lax.optimization_barrier((got_d, att_before1, att_after1))
    state, att_before1, att_after1 = lax.optimization_barrier((state, att_before1, att_after1))
    buckets_here = ROUNDS * BUCKETS
    probability, probability_turned, _ = on_device(
        recall,
        [((buckets_here, SLOTS, SLOTS), F32), ((buckets_here, SLOTS, SLOTS), BF), ((8, TOK), F32)],
        cost=(2 * buckets_here * SLOTS * SLOTS * DIM, 8 << 20, buckets_here * SLOTS * SLOTS),
    )(got_b, state)
    msg, mark = on_device(
        attend_back,
        [((NG, ROWS_E, DIM), BF), ((8, TOK), F32)],
        [((NG, ROWS_C, DIM), BF), pltpu.SemaphoreType.DMA((3,))],
        hbm_in=1,
    )(got_d, got_b, probability, probability_turned, both_gw)
    got_e = exchange(msg, PLANES)
    late_before1, late_after1 = after((att_before1, att_after1), mark)
    att_before2, att_after2 = ring_round(late_before1, late_after1)
    att_before3, att_after3 = ring_round(att_before2, att_after2)
    att_before4 = pass_on(att_before3, 1)
    all_attended = [attended, att_before1, att_before2, att_before3, att_before4]
    all_attended += [att_after3, att_after2, att_after1]
    own_rows, other_rows = on_device(
        project,
        [((NZ * TOK, DIM), F32), ((NZ * TOK, DIM), F32)],
        [
            ((NG, ROWS_D - ROW_PLANE, DIM), BF),
            ((NZ * TOK, width), BF),
            pltpu.SemaphoreType.DMA,
            pltpu.SemaphoreType.DMA((NZ,)),
        ],
        scalars=1,
        hbm_in=1 + NZ,
    )(jnp.stack([core, z_place]), got_d, *all_attended)
    other_rows = swap_cores(other_rows)
    (msg,) = on_device(
        gather_home,
        [((NZ, ROWS_F, DIM), BF)],
        [
            ((NZ, ROUNDS * SLOTS, 2 * DIM), BF),
            ((16 + TOK, TOK), F32),
            ((NZ * TOK, DIM), F32),
            ((NZ * TOK, DIM), F32),
            pltpu.SemaphoreType.DMA((3,)),
        ],
        hbm_in=3,
    )(slots, own_rows, other_rows, got_e)
    got_f = exchange(msg, RINGS)
    grad_qk, grad_values, mixed, grad_weight = on_device(
        unpack_ring,
        [((TOK, width), BF), ((TOK, width), BF), ((TOK, width), BF), ((16, width), F32)],
    )(got_f)
    return (mixed, grad_qk, grad_values, grad_weight)


def solution(mesh):
    assert mesh.shape["ctx"] == NX * NY * NZ and mesh.shape["head"] == 2
    in_specs = (
        P("ctx", "head"),
        P("ctx", "head"),
        P("ctx", "head"),
        P("ctx", "head"),
        P(None, "ctx"),
    )
    out_specs = (P("ctx", "head"), P("ctx", "head"), P("ctx", "head"), P("ctx", "head"))
    return jax.shard_map(
        per_device, mesh=mesh, in_specs=in_specs, out_specs=out_specs, check_vma=False
    )
```

```python
import math

import jax
import jax.numpy as jnp
from jax import lax
from jax.experimental import pallas as pl
from jax.experimental.pallas import tpu as pltpu
from jax.sharding import PartitionSpec as P

NX, NZ, NY = 4, 8, 4
NG = NX * NY
TOK = 128
DIM = 128
ROUNDS = 2
BUCKETS = 8
SLOTS = 256
SCALE = DIM ** (-0.5)
SELF_PENALTY = 10000.0
MASKED = -1e30
BF = jnp.bfloat16
F32 = jnp.float32


def ctx_of(x, z, y):
    return (x * NZ + z) * NY + y


RINGS = [[ctx_of(x, z, y) for z in range(NZ)] for x in range(NX) for y in range(NY)]
PLANES = [[ctx_of(x, z, y) for x in range(NX) for y in range(NY)] for z in range(NZ)]

ROW_W = 512
ROW_LIVE = 640
ROWS_B = 656
ROW_EXTRA = 256
ROWS_C = 272
ROW_PLANE = 272
ROWS_D = 400
ROW_GW = 512
ROWS_E = 640
ROWS_A = 288
ROWS_F = 416


def iota(shape, dim):
    return lax.broadcasted_iota(jnp.int32, shape, dim)


def fiota(shape, dim):
    return iota(shape, dim).astype(F32)


def dot(a, b):
    return jnp.dot(a, b, preferred_element_type=F32)


def dot_nt(a, b):
    return lax.dot_general(a, b, (((1,), (1,)), ((), ())), preferred_element_type=F32)


def dot_tn(a, b):
    return lax.dot_general(a, b, (((0,), (0,)), ((), ())), preferred_element_type=F32)


def ones_where(mask):
    return jnp.where(mask, 1.0, 0.0).astype(BF)


def swap_matrix():
    dest = iota((TOK, TOK), 0)
    source = ((dest >> 1) & 7) * 16 + (dest >> 4) * 2 + (dest & 1)
    return ones_where(iota((TOK, TOK), 1) == source)


def three_parts(spread, lane):
    high = spread.astype(BF).astype(F32)
    rest = spread - high
    middle = rest.astype(BF).astype(F32)
    low = rest - middle
    return jnp.where(lane < 16, high, jnp.where(lane < 32, middle, jnp.where(lane < 48, low, 0.0)))


def split_slot(slot):
    owner = jnp.floor(slot * (1.0 / 16.0))
    inside = slot - 16.0 * owner
    bucket = jnp.floor(inside * 0.5)
    return owner, bucket, inside - 2.0 * bucket


def pack_ring(qk_in, v_in, w_in, b_in, msg_ref, qk_ref, v_ref, w_ref, b_ref, sems):
    fetches = [
        pltpu.make_async_copy(source, dest, sems.at[n])
        for n, (source, dest) in enumerate(((qk_in, qk_ref), (v_in, v_ref), (w_in, w_ref), (b_in, b_ref)))
    ]
    for fetch in fetches:
        fetch.start()
    fetches[3].wait()
    rows = jnp.concatenate([b_ref[...].astype(F32), jnp.zeros((14, TOK), F32)], axis=0).astype(BF)
    for z in range(NZ):
        msg_ref[z, 272:288, :] = rows
    for fetch, ref, span in zip(fetches, (qk_ref, v_ref, w_ref), ((0, 128), (128, 256), (256, 272))):
        fetch.wait()
        for z in range(NZ):
            msg_ref[z, slice(*span), :] = ref[:, z * DIM : (z + 1) * DIM]


def route(a_ref, slot_out, msg_out, slot_ref, y_ref, msg_ref, sems):
    sub = iota((TOK, TOK), 0)
    lane = iota((TOK, TOK), 1)
    swap = swap_matrix()
    slot_sub = fiota((SLOTS, TOK), 0)
    live = jnp.zeros((SLOTS, TOK), F32)
    scols = jnp.zeros((TOK, TOK), F32)
    for z in range(NZ):
        rows = jnp.concatenate([a_ref[z, 0:128, :], a_ref[z, 128:256, :]], axis=1)
        places, marks = [], []
        for r in range(ROUNDS):
            brow = a_ref[z, 272:288, :].astype(F32)[r : r + 1, :]
            bcol = jnp.sum(jnp.where(sub == lane, brow, 0.0), axis=1, keepdims=True)
            same = jnp.where(bcol == brow, 1.0, 0.0)
            prow = jnp.sum(jnp.where(sub < lane, same, 0.0), axis=0, keepdims=True)
            pcol = jnp.sum(jnp.where(lane < sub, same, 0.0), axis=1, keepdims=True)
            srow = 2.0 * brow + prow
            scol = 2.0 * bcol + pcol
            slot_ref[r * NZ + z : r * NZ + z + 1, :] = srow
            scols = jnp.where(lane == r * NZ + z, scol, scols)
            y_ref[r, z] = dot(ones_where(slot_sub == srow), rows).astype(BF)
            owner, _, _ = split_slot(srow)
            places.append(ones_where(slot_sub == owner * 16.0 + (2.0 * z) + prow))
            _, bucket, _ = split_slot(scol)
            marks.append(ones_where(lane.astype(F32) == bucket + (1.0 * r * BUCKETS)))
        live = live + dot(jnp.concatenate(places, axis=1), jnp.concatenate(marks, axis=0))
    slot_ref[16:144, :] = scols
    keeps = [pltpu.make_async_copy(slot_ref, slot_out, sems.at[NG])]
    keeps[0].start()
    live = live.astype(BF)
    for o in range(NG):
        for r in range(ROUNDS):
            block = y_ref[r, :, o * 16 : (o + 1) * 16, :].reshape(TOK, 2 * DIM)
            moved = dot(swap, block).astype(BF)
            msg_ref[o, r * 128 : (r + 1) * 128, :] = moved[:, :DIM]
            msg_ref[o, 256 + r * 128 : 256 + (r + 1) * 128, :] = moved[:, DIM:]
        msg_ref[o, ROW_LIVE:ROWS_B, :] = live[o * 16 : (o + 1) * 16, :]
        for z in range(NZ):
            msg_ref[o, ROW_W + z * 16 : ROW_W + (z + 1) * 16, :] = a_ref[z, 256:272, :]
        keeps.append(pltpu.make_async_copy(msg_ref.at[o], msg_out.at[o], sems.at[o]))
        keeps[-1].start()
    for keep in keeps:
        keep.wait()


def raw_scores(q):
    scores = dot_nt(q, q) * SCALE
    itself = iota((SLOTS, SLOTS), 0) == iota((SLOTS, SLOTS), 1)
    return jnp.where(itself, scores - SELF_PENALTY, scores)


def bucket_rows(ref, start):
    return ref[:, start : start + 16, :].reshape(SLOTS, DIM)


def attend(b_ref, state_out, msg_ref, w_ref, state_ref, sem):
    lane = iota((SLOTS, TOK), 1)
    live = bucket_rows(b_ref, ROW_LIVE)

    def order(j):
        return (j >> 6) * 64 + ((j >> 1) & 7) * 8 + ((j >> 4) & 3) * 2 + (j & 1)

    earlier = ones_where(order(iota((SLOTS, SLOTS), 1)) < order(iota((SLOTS, SLOTS), 0)))
    rank = dot(earlier, live)
    span = jnp.where(rank >= 128.0, 1.0, 0.0)
    kcol = jnp.where(live.astype(F32) > 0.5, span, 2.0).astype(BF)
    pick = ones_where(iota((16, TOK), 0) == iota((16, TOK), 1))
    krows = dot_nt(pick, kcol)
    logs = jnp.zeros((SLOTS, TOK), F32)
    for r in range(ROUNDS):
        for k in range(BUCKETS):
            n = r * BUCKETS + k
            q = bucket_rows(b_ref, r * 128 + k * 16)
            v = bucket_rows(b_ref, 256 + r * 128 + k * 16)
            scores = jnp.where(krows[n : n + 1, :] <= span[:, n : n + 1], raw_scores(q), MASKED)
            largest = jnp.max(scores, axis=1, keepdims=True)
            lifted = jnp.exp(scores - largest)
            summed = jnp.sum(lifted, axis=1, keepdims=True)
            probability = (lifted * (1.0 / summed)).astype(BF)
            out = dot(probability, v).astype(BF)
            msg_ref[:, r * 128 + k * 16 : r * 128 + (k + 1) * 16, :] = out.reshape(NG, 16, DIM)
            logs = jnp.where((lane & 15) == n, largest + jnp.log(summed), logs)
    shifted = dot_nt(span.astype(BF), ones_where(iota((TOK, TOK), 0) == iota((TOK, TOK), 1) + 16))
    state_ref[0:256, :] = jnp.where(lane < 16, logs, shifted)
    state_ref[256:272, :] = krows[:, 0:128]
    state_ref[272:288, :] = krows[:, 128:256]
    keep = pltpu.make_async_copy(state_ref, state_out, sem)
    keep.start()
    msg_ref[:, ROW_EXTRA:ROWS_C, :] = three_parts(logs, lane).astype(BF).reshape(NG, 16, DIM)
    for x in range(NX):
        for y in range(NY):
            for z in range(NZ):
                at = ctx_of(x, z, y) * 16
                w_ref[at : at + 16, :] = b_ref[x * NY + y, ROW_W + z * 16 : ROW_W + (z + 1) * 16, :]
    keep.wait()


def recall(b_ref, state_ref, prob_ref, turned_ref, mark_ref):
    krows = jnp.concatenate([state_ref[256:272, :], state_ref[272:288, :]], axis=1)
    for n in range(ROUNDS * BUCKETS):
        q = bucket_rows(b_ref, n * 16)
        seen = krows[n : n + 1, :] <= state_ref[0:256, 16 + n : 17 + n]
        scores = jnp.where(seen, raw_scores(q), MASKED)
        probability = jnp.exp(scores - state_ref[0:256, n : n + 1])
        prob_ref[n] = probability
        turned_ref[n] = probability.T.astype(BF)
    mark_ref[...] = krows[0:8, 0:128]


def combine(
    z_ref, slot_in, weight_in, c_ref, grad_ref, turned_out, msg_out, att_ref,
    y_ref, s_ref, slot_ref, weight_ref, turned_ref, msg_ref, sems,
):
    fetch = pltpu.make_async_copy(slot_in, slot_ref, sems.at[NZ])
    fetch.start()
    fetch_weight = pltpu.make_async_copy(weight_in, weight_ref, sems.at[NZ + 1])
    fetch_weight.start()
    keeps = []
    lane = iota((TOK, TOK), 1)
    swap = swap_matrix()
    slot_sub = fiota((SLOTS, TOK), 0)
    slot_lane = fiota((TOK, SLOTS), 1)
    for o in range(NG):
        rows = jnp.concatenate([c_ref[o, 0:128, :], c_ref[o, 128:256, :]], axis=1)
        y_ref[:, o * 16 : (o + 1) * 16, :] = dot(swap, rows).astype(BF).reshape(NZ, 16, 2 * DIM)
    log_rows = bucket_rows(c_ref, ROW_EXTRA)
    extra = jnp.zeros((SLOTS, TOK), F32)
    folded = (lane & 15).astype(F32)
    fetch.wait()
    for z in range(NZ):
        outs, logs, marks = [], [], []
        for r in range(ROUNDS):
            n = r * NZ + z
            scol = slot_ref[16:144, n : n + 1]
            outs.append(dot(ones_where(slot_lane == scol), y_ref[z, :, r * DIM : (r + 1) * DIM]))
            owner, bucket, place = split_slot(scol)
            parts = dot(ones_where(slot_lane == owner * 16.0 + (2.0 * z) + place), log_rows)
            marks.append(folded == bucket + (1.0 * r * BUCKETS))
            logs.append(jnp.sum(jnp.where(marks[r], parts, 0.0), axis=1, keepdims=True))
        largest = jnp.maximum(logs[0], logs[1])
        lifted = [jnp.exp(log - largest) for log in logs]
        total = lifted[0] + lifted[1]
        weights = [one / total for one in lifted]
        att = (weights[0] * outs[0] + weights[1] * outs[1]).astype(BF)
        att_ref[z * TOK : (z + 1) * TOK, :] = att
        turned = pl.ds(pl.multiple_of(lax.rem(z_ref[0] - z + NZ, NZ) * TOK, TOK), TOK)
        turned_ref[z * TOK : (z + 1) * TOK, :] = att
        keeps.append(
            pltpu.make_async_copy(turned_ref.at[z * TOK : (z + 1) * TOK, :], turned_out.at[turned, :], sems.at[z])
        )
        keeps[-1].start()
        grad = grad_ref[turned, :]
        inner = jnp.sum(grad * att.astype(F32), axis=1, keepdims=True)
        for r in range(ROUNDS):
            n = r * NZ + z
            srow = slot_ref[n : n + 1, :]
            query_grad = (weights[r] * grad).astype(BF)
            s_ref[z, :, r * DIM : (r + 1) * DIM] = dot(ones_where(slot_sub == srow), query_grad).astype(BF)
            owner, _, place = split_slot(srow)
            spread = jnp.where(marks[r], weights[r] * inner, 0.0)
            extra = extra + dot(
                ones_where(slot_sub == owner * 16.0 + (2.0 * z) + place),
                three_parts(spread, lane).astype(BF),
            )
    fetch_weight.wait()
    extra = extra.astype(BF)
    for o in range(NG):
        moved = dot(swap, s_ref[:, o * 16 : (o + 1) * 16, :].reshape(TOK, 2 * DIM)).astype(BF)
        msg_ref[o, 0:128, :] = moved[:, :DIM]
        msg_ref[o, 128:256, :] = moved[:, DIM:]
        msg_ref[o, ROW_EXTRA:ROWS_C, :] = extra[o * 16 : (o + 1) * 16, :]
        for h in range(NZ):
            msg_ref[o, ROW_PLANE + h * 16 : ROW_PLANE + (h + 1) * 16, :] = weight_ref[:, h * DIM : (h + 1) * DIM]
        keeps.append(pltpu.make_async_copy(msg_ref.at[o], msg_out.at[o], sems.at[NZ + 2 + o]))
        keeps[-1].start()
    for keep in keeps:
        keep.wait()


def attend_back(d_in, b_ref, prob_ref, turned_ref, gw_ref, msg_ref, mark_ref, d_ref, sems):
    fetches = [
        pltpu.make_async_copy(d_in.at[:, rows, :], d_ref.at[:, rows, :], sems.at[n])
        for n, rows in enumerate((slice(ROW_EXTRA, ROWS_C), slice(0, 128), slice(128, 256)))
    ]
    for fetch in fetches:
        fetch.start()
    for x in range(NX):
        for y in range(NY):
            for z in range(NZ):
                at = ctx_of(x, z, y) * 16
                msg_ref[x * NY + y, ROW_GW + z * 16 : ROW_GW + (z + 1) * 16, :] = gw_ref[at : at + 16, :]
    lane = iota((SLOTS, TOK), 1)
    fetches[0].wait()
    shifts = bucket_rows(d_ref, ROW_EXTRA).astype(F32)
    for r in range(ROUNDS):
        fetches[1 + r].wait()
        for k in range(BUCKETS):
            n = r * BUCKETS + k
            q = bucket_rows(b_ref, n * 16)
            v = bucket_rows(b_ref, 256 + n * 16)
            g = bucket_rows(d_ref, n * 16)
            shift = jnp.sum(jnp.where((lane & 15) == n, shifts, 0.0), axis=1, keepdims=True)
            score_grad = (prob_ref[n] * (dot_nt(g, v) - shift)).astype(BF)
            qk_grad = (dot(score_grad, q) + dot_tn(score_grad, q)) * SCALE
            value_grad = dot(turned_ref[n], g)
            msg_ref[:, n * 16 : (n + 1) * 16, :] = qk_grad.astype(BF).reshape(NG, 16, DIM)
            rows = slice(256 + n * 16, 256 + (n + 1) * 16)
            msg_ref[:, rows, :] = value_grad.astype(BF).reshape(NG, 16, DIM)
    mark_ref[...] = shifts[0:8, :]


def join(*refs):
    out_ref, sems = refs[NZ:]
    copies = [
        pltpu.make_async_copy(ref, out_ref.at[n * TOK : (n + 1) * TOK, :], sems.at[n])
        for n, ref in enumerate(refs[:NZ])
    ]
    for copy in copies:
        copy.start()
    for copy in copies:
        copy.wait()


def project(place_ref, d_ref, *refs):
    own_out, other_out, plane_ref, att_ref, sem, sems = refs[NZ:]
    fetch = pltpu.make_async_copy(d_ref.at[:, ROW_PLANE:ROWS_D, :], plane_ref, sem)
    fetch.start()
    blocks = [
        pltpu.make_async_copy(ref, att_ref.at[:, n * DIM : (n + 1) * DIM], sems.at[n])
        for n, ref in enumerate(refs[:NZ])
    ]
    for block in blocks:
        block.start()
    fetch.wait()
    weights = []
    for core in (place_ref[0], 1 - place_ref[0]):
        parts = []
        for turn in range(NZ):
            head = lax.rem(place_ref[1] - turn + NZ, NZ)
            rows = pl.ds(pl.multiple_of(head * 16, 16), 16)
            parts.append(plane_ref[pl.ds(core * (NG // 2), NG // 2), rows, :].reshape(NG * 8, DIM))
        weights.append(jnp.concatenate(parts, axis=1))
    weights = jnp.concatenate(weights, axis=0)
    for block in blocks:
        block.wait()
    for z in range(NZ):
        tokens = slice(z * TOK, (z + 1) * TOK)
        both = dot_nt(att_ref[tokens, :], weights)
        own_out[tokens, :] = both[:, :DIM]
        other_out[tokens, :] = both[:, DIM:]


def gather_home(slot_in, mixed_in, e_ref, msg_ref, y_ref, slot_ref, mixed_ref, sems):
    fetches = [
        pltpu.make_async_copy(source, dest, sems.at[n])
        for n, (source, dest) in enumerate(((slot_in, slot_ref), (mixed_in, mixed_ref)))
    ]
    for fetch in fetches:
        fetch.start()
    swap = swap_matrix()
    slot_lane = fiota((TOK, SLOTS), 1)
    for r in range(ROUNDS):
        for o in range(NG):
            rows = jnp.concatenate(
                [
                    e_ref[o, r * 128 : (r + 1) * 128, :],
                    e_ref[o, 256 + r * 128 : 256 + (r + 1) * 128, :],
                ],
                axis=1,
            )
            at = r * SLOTS + o * 16
            y_ref[:, at : at + 16, :] = dot(swap, rows).astype(BF).reshape(NZ, 16, 2 * DIM)
    total = jnp.zeros((TOK, DIM), F32)
    for o in range(NG):
        total = total + e_ref[o, ROW_GW:ROWS_E, :].astype(F32)
    total = total * (1.0 / math.sqrt(NX * NY * NZ * TOK))
    high = total.astype(BF)
    low = (total - high.astype(F32)).astype(BF)
    fetches[0].wait()
    for z in range(NZ):
        picks = [ones_where(slot_lane == slot_ref[16:144, n : n + 1]) for n in (z, NZ + z)]
        rows = dot(jnp.concatenate(picks, axis=1), y_ref[z]).astype(BF)
        msg_ref[z, 0:128, :] = rows[:, :DIM]
        msg_ref[z, 128:256, :] = rows[:, DIM:]
        msg_ref[z, 384:400, :] = high[z * 16 : (z + 1) * 16, :]
        msg_ref[z, 400:416, :] = low[z * 16 : (z + 1) * 16, :]
    fetches[1].wait()
    for z in range(NZ):
        msg_ref[z, 256:384, :] = mixed_ref[z * TOK : (z + 1) * TOK, :]


def unpack_ring(f_ref, qk_ref, v_ref, mixed_ref, gw_ref):
    for z in range(NZ):
        cols = slice(z * DIM, (z + 1) * DIM)
        qk_ref[:, cols] = f_ref[z, 0:128, :]
        v_ref[:, cols] = f_ref[z, 128:256, :]
        gw_ref[:, cols] = f_ref[z, 384:400, :].astype(F32) + f_ref[z, 400:416, :].astype(F32)
    for z in range(0, NZ, 2):
        first, second = f_ref[z, 256:384, :], f_ref[z + 1, 256:384, :]
        for half in range(2):
            cols = slice(half * 512 + z * 64, half * 512 + z * 64 + 128)
            part = slice(half * 64, half * 64 + 64)
            mixed_ref[:, cols] = jnp.concatenate([first[:, part], second[:, part]], axis=1)


def on_device(body, outs, scratch=(), scalars=0, hbm_in=0, hbm_out=0, vmem=24, cost=None, pin=True):
    shapes = [
        pltpu.HBM(shape, kind) if n < hbm_out else jax.ShapeDtypeStruct(shape, kind)
        for n, (shape, kind) in enumerate(outs)
    ]
    scratches = [pltpu.VMEM(*one) if isinstance(one, tuple) else one for one in scratch]

    def call(*operands):
        operands = [
            pltpu.with_memory_space_constraint(one, pltpu.HBM) if pin and scalars <= n < scalars + hbm_in else one
            for n, one in enumerate(operands)
        ]
        places = [pltpu.SMEM] * scalars + [pltpu.HBM] * hbm_in
        places += [pltpu.VMEM] * (len(operands) - len(places))
        return pl.pallas_call(
            body,
            out_shape=shapes,
            in_specs=[pl.BlockSpec(memory_space=place) for place in places],
            out_specs=[
                pl.BlockSpec(memory_space=pltpu.HBM if n < hbm_out else pltpu.VMEM) for n in range(len(shapes))
            ],
            scratch_shapes=scratches,
            cost_estimate=None if cost is None else pl.CostEstimate(
                flops=cost[0], bytes_accessed=cost[1], transcendentals=cost[2]
            ),
            compiler_params=pltpu.CompilerParams(vmem_limit_bytes=vmem * 1024 * 1024),
        )(*operands)

    return call


def exchange(message, groups):
    return lax.all_to_all(
        message, "ctx", split_axis=0, concat_axis=0, tiled=True, axis_index_groups=groups
    )


def swap_cores(array):
    return lax.ppermute(array, "head", [(0, 1), (1, 0)])


def pass_on(block, step):
    turn = [
        (ctx_of(x, z, y), ctx_of(x, (z + step) % NZ, y)) for x in range(NX) for z in range(NZ) for y in range(NY)
    ]
    return lax.ppermute(block, "ctx", turn)


def ring_round(forward, backward):
    return pass_on(forward, 1), pass_on(backward, -1)


def after(arrays, event):
    return lax.optimization_barrier((*arrays, event))[: len(arrays)]


def per_device(shared_qk, values, out_grad, out_weight, buckets):
    core = lax.axis_index("head")
    z_place = lax.rem(lax.axis_index("ctx") // NY, NZ)
    width = shared_qk.shape[1]

    (msg,) = on_device(
        pack_ring,
        [((NZ, ROWS_A, DIM), BF)],
        [
            ((TOK, width), BF),
            ((TOK, width), BF),
            ((16, width), BF),
            (buckets.shape, jnp.int32),
            pltpu.SemaphoreType.DMA((4,)),
        ],
        hbm_in=4,
    )(shared_qk, values, out_weight, buckets)
    got_a = exchange(msg, RINGS)
    slots, msg = on_device(
        route,
        [((16 + TOK, TOK), F32), ((NG, ROWS_B, DIM), BF)],
        [
            ((16 + TOK, TOK), F32),
            ((ROUNDS, NZ, SLOTS, 2 * DIM), BF),
            ((NG, ROWS_B, DIM), BF),
            pltpu.SemaphoreType.DMA((NG + 1,)),
        ],
        hbm_out=2,
    )(got_a)
    late_grad, msg = lax.optimization_barrier((out_grad, msg))
    got_b = exchange(msg, PLANES)
    before1, after1 = ring_round(late_grad, late_grad)
    before2, after2 = ring_round(before1, after1)
    before3, after3 = ring_round(before2, after2)
    before4 = pass_on(before3, 1)
    blocks = [late_grad, before1, before2, before3, before4, after3, after2, after1]
    (ring_grad,) = on_device(
        join, [((NZ * TOK, width), BF)], [pltpu.SemaphoreType.DMA((NZ,))], hbm_in=NZ, hbm_out=1, pin=False
    )(*blocks)
    state, msg, head_weight = on_device(
        attend,
        [((SLOTS + 32, TOK), F32), ((NG, ROWS_C, DIM), BF), ((2 * width, DIM), BF)],
        [((SLOTS + 32, TOK), F32), pltpu.SemaphoreType.DMA],
        hbm_out=1,
    )(got_b)
    got_c = exchange(msg, PLANES)
    other_grad = swap_cores(ring_grad)
    own_part = lax.dynamic_slice_in_dim(head_weight, core * width, width, 0)
    other_part = lax.dynamic_slice_in_dim(head_weight, (1 - core) * width, width, 0)
    attended_grad = dot(ring_grad, own_part) + dot(other_grad, other_part)
    turned, msg, attended = on_device(
        combine,
        [((NZ * TOK, DIM), BF), ((NG, ROWS_D, DIM), BF), ((NZ * TOK, DIM), BF)],
        [
            ((NZ, SLOTS, 2 * DIM), BF),
            ((NZ, SLOTS, 2 * DIM), BF),
            ((16 + TOK, TOK), F32),
            ((16, width), BF),
            ((NZ * TOK, DIM), BF),
            ((NG, ROWS_D, DIM), BF),
            pltpu.SemaphoreType.DMA((NZ + 2 + NG,)),
        ],
        scalars=1,
        hbm_in=2,
        hbm_out=2,
    )(z_place.reshape(1), slots, out_weight, got_c, attended_grad)
    got_d = exchange(msg, PLANES)
    att_before1, att_after1 = ring_round(attended, attended)
    att_before2, att_after2 = ring_round(att_before1, att_after1)
    own_gw = dot_tn(ring_grad, turned).astype(BF)
    other_gw = dot_tn(other_grad, turned).astype(BF)
    both_gw = jnp.concatenate(
        [jnp.where(core == 0, own_gw, other_gw), jnp.where(core == 0, other_gw, own_gw)], axis=0
    )
    got_d, att_before2, att_after2 = lax.optimization_barrier((got_d, att_before2, att_after2))
    state, att_before2, att_after2 = lax.optimization_barrier((state, att_before2, att_after2))
    buckets_here = ROUNDS * BUCKETS
    probability, probability_turned, _ = on_device(
        recall,
        [((buckets_here, SLOTS, SLOTS), F32), ((buckets_here, SLOTS, SLOTS), BF), ((8, TOK), F32)],
        cost=(2 * buckets_here * SLOTS * SLOTS * DIM, 8 << 20, buckets_here * SLOTS * SLOTS),
    )(got_b, state)
    msg, mark = on_device(
        attend_back,
        [((NG, ROWS_E, DIM), BF), ((8, TOK), F32)],
        [((NG, ROWS_C, DIM), BF), pltpu.SemaphoreType.DMA((3,))],
        hbm_in=1,
    )(got_d, got_b, probability, probability_turned, both_gw)
    got_e = exchange(msg, PLANES)
    late_before2, late_after2 = after((att_before2, att_after2), mark)
    att_before3, att_after3 = ring_round(late_before2, late_after2)
    att_before4 = pass_on(att_before3, 1)
    all_attended = [attended, att_before1, att_before2, att_before3, att_before4]
    all_attended += [att_after3, att_after2, att_after1]
    own_rows, other_rows = on_device(
        project,
        [((NZ * TOK, DIM), F32), ((NZ * TOK, DIM), F32)],
        [
            ((NG, ROWS_D - ROW_PLANE, DIM), BF),
            ((NZ * TOK, width), BF),
            pltpu.SemaphoreType.DMA,
            pltpu.SemaphoreType.DMA((NZ,)),
        ],
        scalars=1,
        hbm_in=1 + NZ,
    )(jnp.stack([core, z_place]), got_d, *all_attended)
    mixed_rows = (own_rows + swap_cores(other_rows)).astype(BF)
    (msg,) = on_device(
        gather_home,
        [((NZ, ROWS_F, DIM), BF)],
        [
            ((NZ, ROUNDS * SLOTS, 2 * DIM), BF),
            ((16 + TOK, TOK), F32),
            ((NZ * TOK, DIM), BF),
            pltpu.SemaphoreType.DMA((2,)),
        ],
        hbm_in=2,
    )(slots, mixed_rows, got_e)
    got_f = exchange(msg, RINGS)
    grad_qk, grad_values, mixed, grad_weight = on_device(
        unpack_ring,
        [((TOK, width), BF), ((TOK, width), BF), ((TOK, width), BF), ((16, width), F32)],
    )(got_f)
    return (mixed, grad_qk, grad_values, grad_weight)


def solution(mesh):
    assert mesh.shape["ctx"] == NX * NY * NZ and mesh.shape["head"] == 2
    in_specs = (
        P("ctx", "head"),
        P("ctx", "head"),
        P("ctx", "head"),
        P("ctx", "head"),
        P(None, "ctx"),
    )
    out_specs = (P("ctx", "head"), P("ctx", "head"), P("ctx", "head"), P("ctx", "head"))
    return jax.shard_map(
        per_device, mesh=mesh, in_specs=in_specs, out_specs=out_specs, check_vma=False
    )
```
